512 devices in a mesh: tile: 32 (over y, z_hi, core), mem: 16 (over x, z_lo).
Axes of the slice: x: 4, y: 4, z: 16 (z_hi: 4, z_lo: 4; z = z_hi * 4 + z_lo), core: 2. Of those that a mesh axis runs over, the one named last changes fastest.
Arguments:
- alpha: float32 [64, 4, 512, 512], P('mem', None, 'tile'), may hold values from -6 to 6
- perturbs: bfloat16 [64, 4, 512, 512], P('mem', None, 'tile'), may hold values from -6 to 6
- diff_x: float32 [64], P('mem'), may hold values from 0.04 to 0.24
- diff_y: float32 [64], P('mem'), may hold values from 0.04 to 0.24
- land_mask: int32 [512, 512], P('tile'), may hold values 0 or 1
- obs_tile: int32 [131072, 1], P(('tile', 'mem')), may hold values from 0 to 31; in each aligned block of 256 rows (0 to 255, 256 to 511, ...) at most 16 rows name the same one
- obs_row: int32 [131072], P(('tile', 'mem')), may hold values from 0 to 14
- obs_col: int32 [131072], P(('tile', 'mem')), may hold values from 0 to 510
- obs_lev: int32 [131072], P(('tile', 'mem')), may hold values from 0 to 3
- obs_weights: float32 [4, 131072], P(None, ('tile', 'mem')), may hold values from 0.1 to 1
- obs_value: float32 [131072], P(('tile', 'mem')), may hold values from -6 to 6
- obs_rinv: float32 [131072], P(('tile', 'mem')), may hold values from 1 to 16
Outputs:
- grad: float32 [64, 4, 512, 512], P('mem', None, 'tile')
- hofx: float32 [131072], P(('tile', 'mem'))
The draws below stay inside these ranges and needn't reach their ends.
Inputs may be any that keep to these rules, and one draw needn't show every extreme that they name: `obs_tile`: among the 256 observations of one device (aligned blocks of rows) no tile is named more than 16 times, a bound that some block reaches.
All inputs are finite; a program needn't handle non-finite values. No bound on the sum of `land_mask` on one device may be relied on, other than what follows from the above.
Results may differ from the reference program's by a relative error of at most 0.00055.
Values sent between devices are 32-bit elements; how exact they have to be, the bound alone decides.
No kernel may reach another device: no remote copies, remote signals or barrier semaphores. Data moves between devices by JAX's collectives and lax.ppermute only.
A program may use at most 64 MiB of HBM per device.

```python
import math
import jax
import jax.numpy as jnp
import numpy as np
from jax import lax

CY = 16
CX = 512
LEV = 4
STEPS = 8
OBS_DEV = 256
MEMBERS = 64
NY = 512
CAP = 16
OBS = 131072
N_TILE = 32


def plant(array, own_key, smallest, top_value):
    dims = array.shape
    index_at = [jax.random.randint(jax.random.fold_in(own_key, axis), (), 0, dims[axis]) for axis in range(len(dims))]
    array = array.at[tuple(index_at)].set(smallest)
    longest = dims.index(max(dims))
    index_at[longest] = (index_at[longest] + 1) % dims[longest]
    return array.at[tuple(index_at)].set(top_value)


def levels(own_key, shape, split, smallest, high):
    loudness, own = 1.0, jax.random.fold_in(own_key, 6)
    for dim, parts in split:
        draws = jnp.exp(jax.random.uniform(jax.random.fold_in(own, dim), (parts,), jnp.float32, smallest / len(split), high / len(split)))
        loudness = loudness * jnp.repeat(draws, shape[dim] // parts).reshape([-1 if axis == dim else 1 for axis in range(len(shape))])
    return loudness


def routed_block(rng, own, number, rows, count, top, limit, skew):
    order = jax.random.permutation(rng, count)
    crowded, common = load_shares(count, rows * top, limit, skew, True), load_shares(count, rows * top, limit, skew, False)
    places = jnp.arange(count)

    def named(sizes, turn):
        used = int((sizes > 0).sum())
        fixed = max(1, used // 4)
        moved = fixed + (places - fixed + turn * (used - fixed)) % max(1, count - fixed)
        return jnp.zeros((count,), jnp.int32).at[order[jnp.where(places < fixed, places, moved)]].set(jnp.asarray(sizes, jnp.int32))

    sizes = jnp.where(number % 4 == 0, named(crowded, number // 4), named(common, number - number // 4 - 1))
    mixed = jax.random.permutation(jax.random.fold_in(own, 3), count)
    donor, receiver = mixed[0:count // 2 * 2:2], mixed[1:count // 2 * 2:2]
    slack = jnp.minimum(sizes[donor] - 1, limit - sizes[receiver]) // 2
    slack = jnp.where((donor == order[0]) | (receiver == order[0]) | (sizes[receiver] == 0), 0, jnp.maximum(slack, 0))
    moved = jax.random.randint(jax.random.fold_in(own, 4), (count // 2,), 0, 1 << 20) % (slack + 1)
    sizes = sizes.at[donor].add(-moved).at[receiver].add(moved)
    members = jnp.searchsorted(jnp.cumsum(sizes), jnp.arange(rows * top), side="right").astype(jnp.int32)
    listing = members.reshape(top, rows).T
    listing = listing[jax.random.permutation(jax.random.fold_in(own, 1), rows)]
    turn = jax.random.randint(jax.random.fold_in(own, 2), (rows, 1), 0, top)
    return jnp.take_along_axis(listing, (jnp.arange(top)[None, :] + turn) % top, axis=1)


def load_shares(count, total, bound, lean, full):
    weights = [(1 << 20) // math.isqrt(grade ** lean) + 1 for grade in range(1, count + 1)]
    largest = bound if full else min(bound, max(-(-total // count), total * weights[0] // sum(weights)))
    least = 1 if total - largest >= count - 1 else 0
    given, rest = [largest] + [least] * (count - 1), total - largest - least * (count - 1)
    while rest > 0:
        candidates = [i for i in range(1, count) if given[i] < largest] or [i for i in range(1, count) if given[i] < bound]
        mass, remaining = sum([weights[i] for i in candidates]), rest
        for i in candidates:
            more = min(bound - given[i], max(1, remaining * weights[i] // mass), rest)
            given[i] = given[i] + more
            rest = rest - more
    return np.array(given)


def bell_draw(own_key, shape, deviation, most, pieces=(), held_as=jnp.bfloat16):
    result = jax.random.normal(own_key, shape, jnp.float32) * deviation
    if len(pieces) > 0:
        result = levels(own_key, shape, pieces, -0.22, 0.18) * result
    return jnp.clip(result, min=-most, max=most).astype(held_as)


def setup_inputs(seed: int = 0) -> dict:
    keys = jax.random.split(jax.random.key(seed), 13)
    alpha = bell_draw(keys[0], (MEMBERS, LEV, NY, CX), 1.0, 6.0, ((0, 16), (2, 32)), jnp.float32)
    perturbs = bell_draw(keys[1], (MEMBERS, LEV, NY, CX), 1.0, 6.0, ((0, 16), (2, 32)))
    diff_x = jnp.clip(jnp.exp(math.log(0.24) - 1.7917595 * jax.random.uniform(keys[2], (MEMBERS,), jnp.float32) ** levels(keys[2], (MEMBERS,), ((0, 16),), -0.2, 0.2)), 0.04, 0.24)
    diff_y = jnp.clip(jnp.exp(math.log(0.24) - 1.7917595 * jax.random.uniform(keys[3], (MEMBERS,), jnp.float32) ** levels(keys[3], (MEMBERS,), ((0, 16),), -0.2, 0.2)), 0.04, 0.24)
    land_mask = plant((jax.random.randint(keys[4], (NY, CX), 0, 5) < 4).astype(jnp.int32), jax.random.fold_in(keys[4], 1), 0, 1)
    obs_tile_keys = jax.random.split(jax.random.fold_in(keys[5], 1), OBS // OBS_DEV)
    obs_tile_turns = jax.random.permutation(jax.random.fold_in(keys[5], 3), OBS // OBS_DEV)
    obs_tile = jax.vmap(lambda own, number: routed_block(jax.random.fold_in(keys[5], 2), own, number, OBS_DEV, N_TILE, 1, CAP, 2))(obs_tile_keys, obs_tile_turns).reshape((OBS, 1))
    obs_row = plant(jax.random.randint(keys[6], (OBS,), 0, CY - 1), jax.random.fold_in(keys[6], 1), 0, (CY - 1) - 1).astype(jnp.int32)
    obs_col = plant(jax.random.randint(keys[7], (OBS,), 0, CX - 1), jax.random.fold_in(keys[7], 1), 0, (CX - 1) - 1).astype(jnp.int32)
    obs_lev = plant(jax.random.randint(keys[8], (OBS,), 0, LEV), jax.random.fold_in(keys[8], 1), 0, LEV - 1).astype(jnp.int32)
    obs_weights = jnp.clip(0.1 + 0.9 * jax.random.uniform(keys[9], (4, OBS), jnp.float32) ** levels(keys[9], (4, OBS), ((1, 512),), -0.2, 0.2), 0.1, 1.0)
    obs_value = bell_draw(keys[10], (OBS,), 1.0, 6.0, ((0, 512),), jnp.float32)
    obs_rinv = jnp.clip(jnp.exp(math.log(16.0) - 2.7725887 * jax.random.uniform(keys[11], (OBS,), jnp.float32) ** levels(keys[11], (OBS,), ((0, 512),), -0.2, 0.2)), 1.0, 16.0)
    return {"alpha": alpha, "perturbs": perturbs, "diff_x": diff_x, "diff_y": diff_y, "land_mask": land_mask, "obs_tile": obs_tile, "obs_row": obs_row, "obs_col": obs_col, "obs_lev": obs_lev, "obs_weights": obs_weights, "obs_value": obs_value, "obs_rinv": obs_rinv}


def smooth(field, rate_x, rate_y):
    for step in range(STEPS):
        padded = jnp.pad(field, ((0, 0), (1, 1), (1, 1)))
        across = padded[:, 1:-1, 2:] + padded[:, 1:-1, :-2] - 2.0 * field
        along = padded[:, 2:, 1:-1] + padded[:, :-2, 1:-1] - 2.0 * field
        field = field + rate_x * across + rate_y * along
    return field

def reference(alpha, perturbs, diff_x, diff_y, land_mask, obs_tile, obs_row, obs_col, obs_lev, obs_weights, obs_value, obs_rinv):
    land = land_mask.astype(jnp.float32)[None]
    factor = (MEMBERS - 1) ** (-0.5)

    def add_member(total, item):
        control, member, rate_x, rate_y = item
        local = land * smooth(land * control, rate_x, rate_y)
        return (total + member.astype(jnp.float32) * local, None)
    start = jnp.zeros((LEV, NY, CX), jnp.float32)
    total, unused = lax.scan(add_member, start, (alpha, perturbs, diff_x, diff_y))
    incr = factor * total
    grow = obs_tile[:, 0].astype(jnp.int32) * CY + obs_row
    index = (obs_lev * NY + grow) * CX + obs_col
    flat = incr.reshape(-1)
    corners = (index, index + 1, index + CX, index + CX + 1)
    hofx = obs_weights[0] * flat[corners[0]]
    for k in range(1, 4):
        hofx = hofx + obs_weights[k] * flat[corners[k]]
    dep = obs_rinv * (hofx - obs_value)
    adjoint = jnp.zeros((LEV * NY * CX,), jnp.float32)
    for k in range(4):
        adjoint = adjoint.at[corners[k]].add(obs_weights[k] * dep)
    adjoint = adjoint.reshape(LEV, NY, CX)

    def member_grad(item):
        control, member, rate_x, rate_y = item
        source = member.astype(jnp.float32) * adjoint
        return control + factor * land * smooth(land * source, rate_x, rate_y)
    grad = lax.map(member_grad, (alpha, perturbs, diff_x, diff_y))
    return (grad, hofx)
```

```python
import functools
import math

import jax
import jax.numpy as jnp
from jax import lax
from jax.experimental import pallas as pl
from jax.experimental.pallas import tpu as pltpu
from jax.sharding import PartitionSpec as P

STEPS = 8
COMPS = 8
LANES = 128
HIGHEST = lax.Precision.HIGHEST
F32 = jnp.float32
BF16 = jnp.bfloat16


def iota(shape, dim):
    return lax.broadcasted_iota(jnp.int32, shape, dim)


def call(body, out_shape, in_specs=None, scratch=(), flops=0, moved=0, name=None):
    return pl.pallas_call(
        body,
        out_shape=out_shape,
        in_specs=in_specs,
        scratch_shapes=scratch,
        compiler_params=pltpu.CompilerParams(vmem_limit_bytes=48 * 2**20),
        cost_estimate=pl.CostEstimate(flops=flops, bytes_accessed=moved, transcendentals=0),
        name=name,
    )


VMEM = pl.BlockSpec(memory_space=pltpu.VMEM)
SMEM = pl.BlockSpec(memory_space=pltpu.SMEM)


def vmem(count):
    return [VMEM] * count


def ranks(tile_row):
    count = tile_row.shape[1]
    along = jnp.broadcast_to(tile_row, (count, count))
    down = along.T
    i, j = iota((count, count), 0), iota((count, count), 1)
    same = along == down
    column = jnp.sum(jnp.where(same & (j < i), 1.0, 0.0), axis=1, keepdims=True)
    row = jnp.sum(jnp.where(same & (i < j), 1.0, 0.0), axis=0, keepdims=True)
    return column, row


def pack_body(tiles, slots, tile_ref, data_ref, send_ref):
    tile_row = tile_ref[...]
    count = tile_row.shape[1]
    column, unused = ranks(tile_row)
    width = COMPS * slots
    expand = jnp.where(iota((COMPS, width), 1) // slots == iota((COMPS, width), 0), 1.0, 0.0)
    data = lax.dot_general(
        data_ref[...], expand, (((0,), (0,)), ((), ())), precision=HIGHEST, preferred_element_type=F32
    )
    slot = (iota((count, width), 1) % slots).astype(F32)
    data = jnp.where(column == slot, data, 0.0)
    choose = jnp.where(iota((tiles, count), 0).astype(F32) == tile_row, 1.0, 0.0)
    send_ref[...] = jnp.dot(choose, data, precision=HIGHEST, preferred_element_type=F32)


def unpack_body(tile_ref, back_ref, hofx_ref):
    tile_row = tile_ref[...]
    tiles, slots = back_ref.shape
    count = tile_row.shape[1]
    unused, row = ranks(tile_row)
    choose = jnp.where(iota((tiles, count), 0).astype(F32) == tile_row, 1.0, 0.0)
    found = lax.dot_general(
        back_ref[...], choose, (((0,), (0,)), ((), ())), precision=HIGHEST, preferred_element_type=F32
    )
    keep = iota((slots, count), 0).astype(F32) == row
    hofx_ref[...] = jnp.sum(jnp.where(keep, found, 0.0), axis=0, keepdims=True)


def rates(group, keep, rate_x_ref, rate_y_ref):
    first = iota((8, LANES), 0) < 4
    rx = jnp.where(first, rate_x_ref[2 * group], rate_x_ref[2 * group + 1])
    ry = jnp.where(first, rate_y_ref[2 * group], rate_y_ref[2 * group + 1])
    centre = 1.0 - 2.0 * rx - 2.0 * ry
    return [(centre * k, rx * k, ry * k) for k in keep]


def smooth_rows(work, rows, coefs, emit):
    total = rows + 2 * STEPS
    parts = work.shape[2] // LANES
    lane = iota((8, LANES), 1)
    at_left, at_right = lane == 0, lane == LANES - 1

    def load(r):
        return [work[r, :, j * LANES : (j + 1) * LANES] for j in range(parts)]

    for step in range(STEPS):
        before, here = load(step), load(step + 1)
        for r in range(step + 1, total - 1 - step):
            after = load(r + 1)
            centre, rx, ry = coefs[0 if r < STEPS else (2 if r >= STEPS + rows else 1)]
            right = [pltpu.roll(v, 1, 1) for v in here]
            left = [pltpu.roll(v, LANES - 1, 1) for v in here]
            new = []
            for j in range(parts):
                low = jnp.where(at_left, right[j - 1] if j > 0 else 0.0, right[j])
                high = jnp.where(at_right, left[j + 1] if j + 1 < parts else 0.0, left[j])
                new.append(centre * here[j] + rx * (low + high) + ry * (before[j] + after[j]))
            if step == STEPS - 1:
                emit(r - STEPS, new)
            else:
                for j in range(parts):
                    work[r, :, j * LANES : (j + 1) * LANES] = new[j]
            before, here = here, after


def tiled(x):
    columns = x.shape[-1]
    x = x.reshape(-1, 8, columns // LANES, LANES)
    return jnp.swapaxes(x, 1, 2).reshape(-1, LANES)


def untiled(x, shape):
    x = x.reshape(-1, shape[-1] // LANES, 8, LANES)
    return jnp.swapaxes(x, 1, 2).reshape(shape)


def at_fields(ref, group, r, j, parts):
    stride = ref.shape[0] // 16
    start = group * 8 * stride + (r // 8 * parts + j) * 8 + r % 8
    return pl.ds(start, 8, stride=stride)


def fields(ref, group, r, j, parts):
    return ref[at_fields(ref, group, r, j, parts), :]


def partial_body(rows, rate_x_ref, rate_y_ref, keep_ref, own_ref, low_ref, high_ref, members_ref, out_ref, work):
    parts = out_ref.shape[1] // LANES
    for group in range(2):
        for j in range(parts):
            lanes = slice(j * LANES, (j + 1) * LANES)
            for r in range(STEPS):
                work[r, :, lanes] = fields(low_ref, group, r, j, parts)
                work[rows + STEPS + r, :, lanes] = fields(high_ref, group, r, j, parts)
            for r in range(rows):
                work[STEPS + r, :, lanes] = fields(own_ref, group, r, j, parts)
        coefs = rates(group, (keep_ref[0], 1.0, keep_ref[1]), rate_x_ref, rate_y_ref)

        def emit(r, new, group=group):
            terms = [new[j] * fields(members_ref, group, r, j, parts) for j in range(parts)]
            if group == 0:
                for j in range(parts):
                    out_ref[r * 8 : r * 8 + 8, j * LANES : (j + 1) * LANES] = terms[j]
                return
            lane, half = iota((8, LANES), 1), iota((8, LANES), 0) < 4
            sums = []
            for j in range(parts):
                both = terms[j] + out_ref[r * 8 : r * 8 + 8, j * LANES : (j + 1) * LANES]
                sums.append(both + pltpu.roll(both, 4, 0))
            left = [pltpu.roll(v, LANES - 1, 1) for v in sums]
            for j in range(parts):
                later = left[j + 1] if j + 1 < parts else left[j]
                shifted = jnp.where(lane == LANES - 1, later, left[j])
                out_ref[r * 8 : r * 8 + 8, j * LANES : (j + 1) * LANES] = jnp.where(
                    half, sums[j], shifted
                )

        smooth_rows(work, rows, coefs, emit)


def grad_body(
    rows,
    factor,
    rate_x_ref,
    rate_y_ref,
    keep_ref,
    alpha_ref,
    land_ref,
    members_ref,
    members_low_ref,
    members_high_ref,
    adjoint_ref,
    adjoint_low_ref,
    adjoint_high_ref,
    out_ref,
    work,
):
    parts = land_ref.shape[1] // LANES

    def twice(ref, r, lanes):
        four = ref[r * 4 : r * 4 + 4, lanes]
        return jnp.concatenate([four, four], axis=0)

    for group in range(2):
        for j in range(parts):
            lanes = slice(j * LANES, (j + 1) * LANES)
            for r in range(STEPS):
                work[r, :, lanes] = fields(members_low_ref, group, r, j, parts) * twice(adjoint_low_ref, r, lanes)
                work[rows + STEPS + r, :, lanes] = fields(members_high_ref, group, r, j, parts) * twice(
                    adjoint_high_ref, r, lanes
                )
            for r in range(rows):
                work[STEPS + r, :, lanes] = (
                    fields(members_ref, group, r, j, parts) * adjoint_ref[r * 8 : r * 8 + 8, lanes]
                )
        coefs = rates(group, (keep_ref[0], 1.0, keep_ref[1]), rate_x_ref, rate_y_ref)

        def emit(r, new, group=group):
            for j in range(parts):
                lanes = slice(j * LANES, (j + 1) * LANES)
                land = jnp.broadcast_to(land_ref[r : r + 1, lanes], (8, LANES)) * factor
                value = fields(alpha_ref, group, r, j, parts) + land * new[j]
                out_ref[at_fields(out_ref, group, r, j, parts), :] = value

        smooth_rows(work, rows, coefs, emit)


def corner_terms(s, slots, comps, scale):
    def comp(k):
        return comps[k * slots + s : k * slots + s + 1, :]

    count = comps.shape[1]
    code = comp(1)
    level = code - 4.0 * jnp.floor(code * 0.25)
    row = jnp.floor(code * 0.25)
    sub = iota((8, count), 0).astype(F32)
    weights = [comp(2 + k) if scale is None else comp(2 + k) * scale for k in range(4)]
    left, right = sub == level, sub == level + 4.0
    lower = jnp.where(left, weights[0], jnp.where(right, weights[1], 0.0))
    upper = jnp.where(left, weights[2], jnp.where(right, weights[3], 0.0))
    return jnp.broadcast_to(row, (8, count)), lower, upper


def interpolate_body(rows, slots, raw_ref, field_ref, comps_ref, out_ref, pieces):
    comps_ref[...] = raw_ref[...].T
    columns = field_ref.shape[1]
    count = comps_ref.shape[1]
    field = field_ref[...]
    top = field.astype(BF16)
    pieces[: 8 * rows, :] = top
    pieces[8 * rows :, :] = (field - top.astype(F32)).astype(BF16)
    for s in range(slots):
        column = comps_ref[s : s + 1, :].astype(jnp.int32)
        hot = jnp.where(iota((columns, count), 0) == column, 1.0, 0.0).astype(BF16)
        found = jnp.dot(pieces[...], hot, preferred_element_type=F32)
        row, lower, upper = corner_terms(s, slots, comps_ref, None)
        total = jnp.zeros((8, count), F32)
        previous = None
        for g in range(rows):
            at = row == float(g)
            value = found[g * 8 : g * 8 + 8] + found[8 * (rows + g) : 8 * (rows + g) + 8]
            rest = 0.0 if previous is None else jnp.where(previous, upper, 0.0)
            total = total + jnp.where(at, lower, rest) * value
            previous = at
        out_ref[s : s + 1, :] = jnp.sum(total, axis=0, keepdims=True)


def spread_body(
    rows, slots, tiles, factor, me_ref, raw_ref, comps_ref, sums_ref, own_ref, low_ref, high_ref, back_ref, left, total
):
    columns = own_ref.shape[1]
    count = comps_ref.shape[1]
    hofx = sums_ref[0]
    for k in range(1, sums_ref.shape[0]):
        hofx = hofx + sums_ref[k]
    hofx = factor * hofx
    mine = iota((tiles, count), 1) == me_ref[0] * tiles + iota((tiles, count), 0)
    back_ref[...] = lax.dot_general(
        jnp.where(mine, 1.0, 0.0),
        hofx,
        (((1,), (1,)), ((), ())),
        precision=HIGHEST,
        preferred_element_type=F32,
    )
    value = comps_ref[6 * slots : 7 * slots, :]
    rinv = comps_ref[7 * slots : 8 * slots, :]
    dep = rinv * (hofx - value)
    for s in range(slots):
        row, lower, upper = corner_terms(s, slots, comps_ref, dep[s : s + 1, :])
        previous = None
        for g in range(rows):
            at = row == float(g)
            rest = 0.0 if previous is None else jnp.where(previous, upper, 0.0)
            term = jnp.where(at, lower, rest)
            top = term.astype(BF16)
            left[g * 8 : g * 8 + 8, :] = top
            left[8 * (rows + g) : 8 * (rows + g) + 8, :] = (term - top.astype(F32)).astype(BF16)
            previous = at
        column = raw_ref[:, s : s + 1].astype(jnp.int32)
        hot = jnp.where(iota((count, columns), 1) == column, 1.0, 0.0).astype(BF16)
        part = jnp.dot(left[...], hot, preferred_element_type=F32)
        if s == 0:
            total[...] = part
        else:
            total[...] += part
    lane, half = iota((8, columns), 1), iota((8, columns), 0) < 4
    for g in range(rows):
        both = total[g * 8 : g * 8 + 8, :] + total[8 * (rows + g) : 8 * (rows + g) + 8, :]
        moved = jnp.where(lane == 0, 0.0, pltpu.roll(pltpu.roll(both, 4, 0), 1, 1))
        four = both + moved
        own_ref[g * 8 : g * 8 + 8, :] = jnp.where(half, four, pltpu.roll(four, 4, 0))
        if g < STEPS:
            low_ref[g * 4 : g * 4 + 4, :] = four[:4]
        if g >= rows - STEPS:
            at = g - (rows - STEPS)
            high_ref[at * 4 : at * 4 + 4, :] = four[:4]


def on_device(
    alpha,
    perturbs,
    diff_x,
    diff_y,
    land_mask,
    obs_tile,
    obs_row,
    obs_col,
    obs_lev,
    obs_weights,
    obs_value,
    obs_rinv,
):
    members, levels, rows, columns = alpha.shape
    tiles, mems = lax.axis_size("tile"), lax.axis_size("mem")
    factor = (mems * members - 1) ** (-0.5)
    slots = 16
    inner = math.isqrt(mems)
    near = [[i * inner + j for j in range(inner)] for i in range(inner)]
    far = [[i * inner + j for i in range(inner)] for j in range(inner)]
    forward = [(i, i + 1) for i in range(tiles - 1)]
    backward = [(i + 1, i) for i in range(tiles - 1)]
    place = lax.axis_index("tile")
    keep = jnp.stack([place > 0, place < tiles - 1]).astype(F32)
    me = lax.axis_index("mem").astype(jnp.int32).reshape(1)
    flat = (members * levels * rows * columns // LANES, LANES)

    def exchange(low_rows, high_rows):
        return lax.ppermute(high_rows, "tile", forward), lax.ppermute(low_rows, "tile", backward)

    land = land_mask.astype(F32)
    own = land * alpha
    low, high = exchange(tiled(own[:, :, :STEPS]), tiled(own[:, :, rows - STEPS :]))
    own = tiled(own)

    tile_row = obs_tile.reshape(1, -1).astype(F32)
    data = jnp.concatenate(
        [
            obs_col.astype(F32)[None],
            (obs_row * levels + obs_lev).astype(F32)[None],
            obs_weights,
            obs_value[None],
            obs_rinv[None],
        ],
        axis=0,
    )
    width = COMPS * slots
    sent = call(
        functools.partial(pack_body, tiles, slots),
        jax.ShapeDtypeStruct((tiles, width), F32),
        vmem(2),
        name="pack",
    )(tile_row, data)
    routed = lax.all_to_all(sent, "tile", split_axis=0, concat_axis=0, tiled=True)
    raw = lax.all_to_all(
        jnp.broadcast_to(routed[None], (mems, tiles, width)), "mem", split_axis=0, concat_axis=0, tiled=True
    ).reshape(mems * tiles, width)

    masked = land * perturbs.astype(F32)
    members_low, members_high = exchange(tiled(masked[:, :, :STEPS]), tiled(masked[:, :, rows - STEPS :]))
    masked = tiled(masked)

    work = pltpu.VMEM((rows + 2 * STEPS, 8, columns), F32)
    partial = call(
        functools.partial(partial_body, rows),
        jax.ShapeDtypeStruct((8 * rows, columns), F32),
        [SMEM] * 3 + vmem(4),
        [work],
        flops=2 * 10**7,
        moved=2 * 10**6,
        name="partial",
    )(diff_x, diff_y, keep, own, low, high, masked)

    count = mems * tiles
    comps, found = call(
        functools.partial(interpolate_body, rows, slots),
        (jax.ShapeDtypeStruct((width, count), F32), jax.ShapeDtypeStruct((slots, count), F32)),
        vmem(2),
        [pltpu.VMEM((16 * rows, columns), BF16)],
        name="interpolate",
    )(raw, partial)

    def gather(x, groups):
        return lax.all_to_all(
            jnp.broadcast_to(x[None], (inner,) + x.shape),
            "mem",
            split_axis=0,
            concat_axis=0,
            axis_index_groups=groups,
            tiled=True,
        )

    sums = gather(jnp.sum(gather(found, near), axis=0), far)
    adjoint, adjoint_first, adjoint_last, back = call(
        functools.partial(spread_body, rows, slots, tiles, factor),
        (
            jax.ShapeDtypeStruct((8 * rows, columns), F32),
            jax.ShapeDtypeStruct((levels * STEPS, columns), F32),
            jax.ShapeDtypeStruct((levels * STEPS, columns), F32),
            jax.ShapeDtypeStruct((tiles, slots), F32),
        ),
        [SMEM] + vmem(3),
        [pltpu.VMEM((16 * rows, count), BF16), pltpu.VMEM((16 * rows, columns), F32)],
        name="spread",
    )(me, raw, comps, sums)
    adjoint_low, adjoint_high = exchange(adjoint_first, adjoint_last)
    returned = lax.all_to_all(back, "tile", split_axis=0, concat_axis=0, tiled=True)

    grad = call(
        functools.partial(grad_body, rows, factor),
        jax.ShapeDtypeStruct(flat, F32),
        [SMEM] * 3 + vmem(8),
        [work],
        flops=2 * 10**7,
        moved=2 * 10**6,
        name="grad",
    )(
        diff_x,
        diff_y,
        keep,
        tiled(alpha),
        land,
        masked,
        members_low,
        members_high,
        adjoint,
        adjoint_low,
        adjoint_high,
    )
    hofx = call(
        unpack_body,
        jax.ShapeDtypeStruct((1, tile_row.shape[1]), F32),
        vmem(2),
        name="unpack",
    )(tile_row, returned)
    return untiled(grad, alpha.shape), hofx.reshape(-1)


def solution(mesh):
    return jax.shard_map(
        on_device,
        mesh=mesh,
        in_specs=(
            P("mem", None, "tile", None),
            P("mem", None, "tile", None),
            P("mem"),
            P("mem"),
            P("tile", None),
            P(("tile", "mem"), None),
            P(("tile", "mem")),
            P(("tile", "mem")),
            P(("tile", "mem")),
            P(None, ("tile", "mem")),
            P(("tile", "mem")),
            P(("tile", "mem")),
        ),
        out_specs=(P("mem", None, "tile", None), P(("tile", "mem"))),
        check_vma=False,
    )
```

```python
import functools
import math

import jax
import jax.numpy as jnp
from jax import lax
from jax.experimental import pallas as pl
from jax.experimental.pallas import tpu as pltpu
from jax.sharding import PartitionSpec as P

STEPS = 8
COMPS = 8
LANES = 128
HIGHEST = lax.Precision.HIGHEST
F32 = jnp.float32
BF16 = jnp.bfloat16
PACK_FLOPS = 10**11
PARTIAL_FLOPS = 10**11


def iota(shape, dim):
    return lax.broadcasted_iota(jnp.int32, shape, dim)


def call(body, out_shape, in_specs=None, scratch=(), flops=0, moved=0, name=None):
    return pl.pallas_call(
        body,
        out_shape=out_shape,
        in_specs=in_specs,
        scratch_shapes=scratch,
        compiler_params=pltpu.CompilerParams(vmem_limit_bytes=48 * 2**20),
        cost_estimate=pl.CostEstimate(flops=flops, bytes_accessed=moved, transcendentals=0),
        name=name,
    )


VMEM = pl.BlockSpec(memory_space=pltpu.VMEM)
SMEM = pl.BlockSpec(memory_space=pltpu.SMEM)


def vmem(count):
    return [VMEM] * count


def ranks(tile_row):
    count = tile_row.shape[1]
    along = jnp.broadcast_to(tile_row, (count, count))
    down = along.T
    i, j = iota((count, count), 0), iota((count, count), 1)
    same = along == down
    column = jnp.sum(jnp.where(same & (j < i), 1.0, 0.0), axis=1, keepdims=True)
    row = jnp.sum(jnp.where(same & (i < j), 1.0, 0.0), axis=0, keepdims=True)
    return column, row


def pack_body(
    tiles, slots, levels, unused_ref, tile_ref, row_ref, col_ref, lev_ref, weights_ref, value_ref, rinv_ref, send_ref, data_ref
):
    tile_row = tile_ref[...].astype(F32)
    data_ref[0:1, :] = col_ref[...].astype(F32)
    data_ref[1:2, :] = (row_ref[...] * levels + lev_ref[...]).astype(F32)
    data_ref[2:6, :] = weights_ref[...]
    data_ref[6:7, :] = value_ref[...]
    data_ref[7:8, :] = rinv_ref[...]
    count = tile_row.shape[1]
    column, unused = ranks(tile_row)
    width = COMPS * slots
    expand = jnp.where(iota((COMPS, width), 1) // slots == iota((COMPS, width), 0), 1.0, 0.0)
    data = lax.dot_general(
        data_ref[...], expand, (((0,), (0,)), ((), ())), precision=HIGHEST, preferred_element_type=F32
    )
    slot = (iota((count, width), 1) % slots).astype(F32)
    data = jnp.where(column == slot, data, 0.0)
    choose = jnp.where(iota((tiles, count), 0).astype(F32) == tile_row, 1.0, 0.0)
    send_ref[...] = jnp.dot(choose, data, precision=HIGHEST, preferred_element_type=F32)


def unpack_body(tile_ref, back_ref, hofx_ref):
    tile_row = tile_ref[...].astype(F32)
    tiles, slots = back_ref.shape
    count = tile_row.shape[1]
    unused, row = ranks(tile_row)
    choose = jnp.where(iota((tiles, count), 0).astype(F32) == tile_row, 1.0, 0.0)
    found = lax.dot_general(
        back_ref[...], choose, (((0,), (0,)), ((), ())), precision=HIGHEST, preferred_element_type=F32
    )
    keep = iota((slots, count), 0).astype(F32) == row
    hofx_ref[...] = jnp.sum(jnp.where(keep, found, 0.0), axis=0, keepdims=True)


def rates(group, keep, rate_x_ref, rate_y_ref):
    first = iota((8, LANES), 0) < 4
    rx = jnp.where(first, rate_x_ref[2 * group], rate_x_ref[2 * group + 1])
    ry = jnp.where(first, rate_y_ref[2 * group], rate_y_ref[2 * group + 1])
    centre = 1.0 - 2.0 * rx - 2.0 * ry
    return [(centre * k, rx * k, ry * k) for k in keep]


def smooth_rows(work, rows, coefs, emit):
    total = rows + 2 * STEPS
    parts = work.shape[2] // LANES
    lane = iota((8, LANES), 1)
    at_left, at_right = lane == 0, lane == LANES - 1

    def load(r):
        return [work[r, :, j * LANES : (j + 1) * LANES] for j in range(parts)]

    for step in range(STEPS):
        before, here = load(step), load(step + 1)
        for r in range(step + 1, total - 1 - step):
            after = load(r + 1)
            centre, rx, ry = coefs[0 if r < STEPS else (2 if r >= STEPS + rows else 1)]
            right = [pltpu.roll(v, 1, 1) for v in here]
            left = [pltpu.roll(v, LANES - 1, 1) for v in here]
            new = []
            for j in range(parts):
                low = jnp.where(at_left, right[j - 1] if j > 0 else 0.0, right[j])
                high = jnp.where(at_right, left[j + 1] if j + 1 < parts else 0.0, left[j])
                new.append(centre * here[j] + rx * (low + high) + ry * (before[j] + after[j]))
            if step == STEPS - 1:
                emit(r - STEPS, new)
            else:
                for j in range(parts):
                    work[r, :, j * LANES : (j + 1) * LANES] = new[j]
            before, here = here, after


def tiled(x):
    columns = x.shape[-1]
    x = x.reshape(-1, 8, columns // LANES, LANES)
    return jnp.swapaxes(x, 1, 2).reshape(-1, LANES)


def untiled(x, shape):
    x = x.reshape(-1, shape[-1] // LANES, 8, LANES)
    return jnp.swapaxes(x, 1, 2).reshape(shape)


def at_fields(base, stride, group, r, j, parts):
    return pl.ds(base + group * 8 * stride + (r // 8 * parts + j) * 8 + r % 8, 8, stride=stride)


def odd_tile():
    return lax.rem(lax.axis_index("tile"), 2)


def keep_sides(tiles):
    place = lax.axis_index("tile")
    return jnp.where(place > 0, 1.0, 0.0), jnp.where(place < tiles - 1, 1.0, 0.0)


def prep_body(alpha_ref, members_ref, land_ref, own_ref, masked_ref, far_ref, near_ref):
    members, levels, rows, columns = members_ref.shape
    parts = columns // LANES
    size = rows * parts
    count = members * levels
    land = land_ref[...].astype(F32)
    for f in range(count):
        field = land * members_ref[f // levels, f % levels].astype(F32)
        for k in range(rows // 8):
            for j in range(parts):
                at = f * size + (k * parts + j) * 8
                mask = land[k * 8 : k * 8 + 8, j * LANES : (j + 1) * LANES]
                own_ref[at : at + 8, :] = mask * alpha_ref[at : at + 8, :]
                masked_ref[at : at + 8, :] = field[k * 8 : k * 8 + 8, j * LANES : (j + 1) * LANES]
    brim = STEPS * parts
    odd = odd_tile()
    first = odd * (size - brim)
    last = (1 - odd) * (size - brim)
    for source, start in ((own_ref, 0), (masked_ref, count * brim)):
        for f in range(count):
            to = slice(start + f * brim, start + (f + 1) * brim)
            far_ref[to, :] = source[pl.ds(pl.multiple_of(f * size + first, 8), brim), :]
            near_ref[to, :] = source[pl.ds(pl.multiple_of(f * size + last, 8), brim), :]


def partial_body(rows, tiles, rate_x_ref, rate_y_ref, own_ref, far_ref, near_ref, members_ref, out_ref, work):
    parts = out_ref.shape[1] // LANES
    size, brim = rows * parts, STEPS * parts
    odd = odd_tile()
    far_at, near_at = odd * (rows + STEPS), (1 - odd) * (rows + STEPS)
    below, above = keep_sides(tiles)
    for group in range(2):
        for j in range(parts):
            lanes = slice(j * LANES, (j + 1) * LANES)
            for r in range(STEPS):
                work[far_at + r, :, lanes] = far_ref[at_fields(0, brim, group, r, j, parts), :]
                work[near_at + r, :, lanes] = near_ref[at_fields(0, brim, group, r, j, parts), :]
            for r in range(rows):
                work[STEPS + r, :, lanes] = own_ref[at_fields(0, size, group, r, j, parts), :]
        coefs = rates(group, (below, 1.0, above), rate_x_ref, rate_y_ref)

        def emit(r, new, group=group):
            terms = [new[j] * members_ref[at_fields(0, size, group, r, j, parts), :] for j in range(parts)]
            if group == 0:
                for j in range(parts):
                    out_ref[r * 8 : r * 8 + 8, j * LANES : (j + 1) * LANES] = terms[j]
                return
            lane, half = iota((8, LANES), 1), iota((8, LANES), 0) < 4
            sums = []
            for j in range(parts):
                both = terms[j] + out_ref[r * 8 : r * 8 + 8, j * LANES : (j + 1) * LANES]
                sums.append(both + pltpu.roll(both, 4, 0))
            left = [pltpu.roll(v, LANES - 1, 1) for v in sums]
            for j in range(parts):
                later = left[j + 1] if j + 1 < parts else left[j]
                shifted = jnp.where(lane == LANES - 1, later, left[j])
                out_ref[r * 8 : r * 8 + 8, j * LANES : (j + 1) * LANES] = jnp.where(
                    half, sums[j], shifted
                )

        smooth_rows(work, rows, coefs, emit)


def grad_body(
    rows,
    tiles,
    factor,
    rate_x_ref,
    rate_y_ref,
    alpha_ref,
    land_ref,
    members_ref,
    far_ref,
    near_ref,
    adjoint_ref,
    adjoint_far_ref,
    adjoint_near_ref,
    out_ref,
    work,
):
    parts = land_ref.shape[1] // LANES
    size, brim = rows * parts, STEPS * parts
    odd = odd_tile()
    far_at, near_at = odd * (rows + STEPS), (1 - odd) * (rows + STEPS)
    below, above = keep_sides(tiles)

    def twice(ref, r, lanes):
        four = ref[r * 4 : r * 4 + 4, lanes]
        return jnp.concatenate([four, four], axis=0)

    for group in range(2):
        for j in range(parts):
            lanes = slice(j * LANES, (j + 1) * LANES)
            for r in range(STEPS):
                at = at_fields(16 * brim, brim, group, r, j, parts)
                work[far_at + r, :, lanes] = far_ref[at, :] * twice(adjoint_far_ref, r, lanes)
                work[near_at + r, :, lanes] = near_ref[at, :] * twice(adjoint_near_ref, r, lanes)
            for r in range(rows):
                own = members_ref[at_fields(0, size, group, r, j, parts), :]
                work[STEPS + r, :, lanes] = own * adjoint_ref[r * 8 : r * 8 + 8, lanes]
        coefs = rates(group, (below, 1.0, above), rate_x_ref, rate_y_ref)

        def emit(r, new, group=group):
            for j in range(parts):
                lanes = slice(j * LANES, (j + 1) * LANES)
                land = jnp.broadcast_to(land_ref[r : r + 1, lanes].astype(F32), (8, LANES)) * factor
                at = at_fields(0, size, group, r, j, parts)
                out_ref[at, :] = alpha_ref[at, :] + land * new[j]

        smooth_rows(work, rows, coefs, emit)


def corner_terms(s, slots, comps, scale):
    def comp(k):
        return comps[k * slots + s : k * slots + s + 1, :]

    count = comps.shape[1]
    code = comp(1)
    level = code - 4.0 * jnp.floor(code * 0.25)
    row = jnp.floor(code * 0.25)
    sub = iota((8, count), 0).astype(F32)
    weights = [comp(2 + k) if scale is None else comp(2 + k) * scale for k in range(4)]
    left, right = sub == level, sub == level + 4.0
    lower = jnp.where(left, weights[0], jnp.where(right, weights[1], 0.0))
    upper = jnp.where(left, weights[2], jnp.where(right, weights[3], 0.0))
    return jnp.broadcast_to(row, (8, count)), lower, upper


def interpolate_body(rows, slots, raw_ref, field_ref, comps_ref, out_ref, pieces):
    comps_ref[...] = raw_ref[...].T
    columns = field_ref.shape[1]
    count = comps_ref.shape[1]
    field = field_ref[...]
    top = field.astype(BF16)
    pieces[: 8 * rows, :] = top
    pieces[8 * rows :, :] = (field - top.astype(F32)).astype(BF16)
    for s in range(slots):
        column = comps_ref[s : s + 1, :].astype(jnp.int32)
        hot = jnp.where(iota((columns, count), 0) == column, 1.0, 0.0).astype(BF16)
        found = jnp.dot(pieces[...], hot, preferred_element_type=F32)
        row, lower, upper = corner_terms(s, slots, comps_ref, None)
        total = jnp.zeros((8, count), F32)
        previous = None
        for g in range(rows):
            at = row == float(g)
            value = found[g * 8 : g * 8 + 8] + found[8 * (rows + g) : 8 * (rows + g) + 8]
            rest = 0.0 if previous is None else jnp.where(previous, upper, 0.0)
            total = total + jnp.where(at, lower, rest) * value
            previous = at
        total = jnp.sum(total, axis=0, keepdims=True)
        for k in range(out_ref.shape[0]):
            out_ref[k, s : s + 1, :] = total


def add_body(in_ref, out_ref):
    total = in_ref[0]
    for k in range(1, in_ref.shape[0]):
        total = total + in_ref[k]
    for k in range(out_ref.shape[0]):
        out_ref[k] = total


def spread_body(
    rows, slots, tiles, factor, raw_ref, comps_ref, sums_ref, own_ref, far_ref, near_ref, back_ref, left, total
):
    columns = own_ref.shape[1]
    count = comps_ref.shape[1]
    hofx = sums_ref[0]
    for k in range(1, sums_ref.shape[0]):
        hofx = hofx + sums_ref[k]
    hofx = factor * hofx
    mine = iota((tiles, count), 1) == lax.axis_index("mem") * tiles + iota((tiles, count), 0)
    back_ref[...] = lax.dot_general(
        jnp.where(mine, 1.0, 0.0),
        hofx,
        (((1,), (1,)), ((), ())),
        precision=HIGHEST,
        preferred_element_type=F32,
    )
    value = comps_ref[6 * slots : 7 * slots, :]
    rinv = comps_ref[7 * slots : 8 * slots, :]
    dep = rinv * (hofx - value)
    for s in range(slots):
        row, lower, upper = corner_terms(s, slots, comps_ref, dep[s : s + 1, :])
        previous = None
        for g in range(rows):
            at = row == float(g)
            rest = 0.0 if previous is None else jnp.where(previous, upper, 0.0)
            term = jnp.where(at, lower, rest)
            top = term.astype(BF16)
            left[g * 8 : g * 8 + 8, :] = top
            left[8 * (rows + g) : 8 * (rows + g) + 8, :] = (term - top.astype(F32)).astype(BF16)
            previous = at
        column = raw_ref[:, s : s + 1].astype(jnp.int32)
        hot = jnp.where(iota((count, columns), 1) == column, 1.0, 0.0).astype(BF16)
        part = jnp.dot(left[...], hot, preferred_element_type=F32)
        if s == 0:
            total[...] = part
        else:
            total[...] += part
    lane, half = iota((8, columns), 1), iota((8, columns), 0) < 4
    for g in range(rows):
        both = total[g * 8 : g * 8 + 8, :] + total[8 * (rows + g) : 8 * (rows + g) + 8, :]
        moved = jnp.where(lane == 0, 0.0, pltpu.roll(pltpu.roll(both, 4, 0), 1, 1))
        four = both + moved
        own_ref[g * 8 : g * 8 + 8, :] = jnp.where(half, four, pltpu.roll(four, 4, 0))
    odd = odd_tile()
    first, last = odd * (rows - STEPS), (1 - odd) * (rows - STEPS)
    for ref, start in ((far_ref, first), (near_ref, last)):
        for r in range(STEPS):
            ref[r * 4 : r * 4 + 4, :] = own_ref[pl.ds(pl.multiple_of((start + r) * 8, 8), 8), :][:4]


def on_device(
    alpha,
    perturbs,
    diff_x,
    diff_y,
    land_mask,
    obs_tile,
    obs_row,
    obs_col,
    obs_lev,
    obs_weights,
    obs_value,
    obs_rinv,
):
    members, levels, rows, columns = alpha.shape
    tiles, mems = lax.axis_size("tile"), lax.axis_size("mem")
    factor = (mems * members - 1) ** (-0.5)
    slots = 16
    inner = math.isqrt(mems)
    near_group = [[i * inner + j for j in range(inner)] for i in range(inner)]
    far_group = [[i * inner + j for i in range(inner)] for j in range(inner)]
    pairs = [(i, i + 1) for i in range(0, tiles - 1, 2)]
    near_pairs = pairs + [(b, a) for a, b in pairs]
    pairs = [(i, i + 1) for i in range(1, tiles - 1, 2)]
    far_pairs = pairs + [(b, a) for a, b in pairs]
    size = members * levels * rows * columns // LANES
    brim = members * levels * STEPS * columns // LANES

    def exchange(far, near):
        return lax.ppermute(far, "tile", far_pairs), lax.ppermute(near, "tile", near_pairs)

    alpha_tiles = tiled(alpha)
    own, masked, far, near = call(
        prep_body,
        (
            jax.ShapeDtypeStruct((size, LANES), F32),
            jax.ShapeDtypeStruct((size, LANES), F32),
            jax.ShapeDtypeStruct((2 * brim, LANES), F32),
            jax.ShapeDtypeStruct((2 * brim, LANES), F32),
        ),
        vmem(3),
        name="prep",
    )(alpha_tiles, perturbs, land_mask)
    halo_far, halo_near = exchange(far, near)

    count = obs_row.shape[0]
    tile_row = obs_tile.reshape(1, count)
    width = COMPS * slots
    sent = call(
        functools.partial(pack_body, tiles, slots, levels),
        jax.ShapeDtypeStruct((tiles, width), F32),
        [pl.BlockSpec(memory_space=pl.ANY)] + vmem(7),
        [pltpu.VMEM((COMPS, count), F32)],
        flops=PACK_FLOPS,
        name="pack",
    )(
        far,
        tile_row,
        obs_row.reshape(1, count),
        obs_col.reshape(1, count),
        obs_lev.reshape(1, count),
        obs_weights,
        obs_value.reshape(1, count),
        obs_rinv.reshape(1, count),
    )
    routed = lax.all_to_all(sent, "tile", split_axis=0, concat_axis=0, tiled=True)
    count = mems * tiles
    raw = lax.all_to_all(
        jnp.broadcast_to(routed[None], (mems, tiles, width)), "mem", split_axis=0, concat_axis=0, tiled=True
    ).reshape(count, width)

    work = pltpu.VMEM((rows + 2 * STEPS, 8, columns), F32)
    partial = call(
        functools.partial(partial_body, rows, tiles),
        jax.ShapeDtypeStruct((8 * rows, columns), F32),
        [SMEM] * 2 + vmem(4),
        [work],
        flops=PARTIAL_FLOPS,
        name="partial",
    )(diff_x, diff_y, own, halo_far, halo_near, masked)
    copies = jax.ShapeDtypeStruct((inner, slots, count), F32)
    comps, found = call(
        functools.partial(interpolate_body, rows, slots),
        (jax.ShapeDtypeStruct((width, count), F32), copies),
        vmem(2),
        [pltpu.VMEM((16 * rows, columns), BF16)],
        name="interpolate",
    )(raw, partial)

    def gather(x, groups):
        return lax.all_to_all(x, "mem", split_axis=0, concat_axis=0, axis_index_groups=groups, tiled=True)

    sums = gather(call(add_body, copies, vmem(1), name="add")(gather(found, near_group)), far_group)
    edge = jax.ShapeDtypeStruct((levels * STEPS, columns), F32)
    adjoint, edge_far, edge_near, back = call(
        functools.partial(spread_body, rows, slots, tiles, factor),
        (
            jax.ShapeDtypeStruct((8 * rows, columns), F32),
            edge,
            edge,
            jax.ShapeDtypeStruct((tiles, slots), F32),
        ),
        vmem(3),
        [pltpu.VMEM((16 * rows, count), BF16), pltpu.VMEM((16 * rows, columns), F32)],
        name="spread",
    )(raw, comps, sums)
    adjoint_far, adjoint_near = exchange(edge_far, edge_near)
    returned = lax.all_to_all(back, "tile", split_axis=0, concat_axis=0, tiled=True)

    grad = call(
        functools.partial(grad_body, rows, tiles, factor),
        jax.ShapeDtypeStruct((size, LANES), F32),
        [SMEM] * 2 + vmem(8),
        [work],
        name="grad",
    )(
        diff_x,
        diff_y,
        alpha_tiles,
        land_mask,
        masked,
        halo_far,
        halo_near,
        adjoint,
        adjoint_far,
        adjoint_near,
    )
    hofx = call(
        unpack_body,
        jax.ShapeDtypeStruct((1, obs_row.shape[0]), F32),
        vmem(2),
        name="unpack",
    )(tile_row, returned)
    return untiled(grad, alpha.shape), hofx.reshape(-1)


def solution(mesh):
    return jax.shard_map(
        on_device,
        mesh=mesh,
        in_specs=(
            P("mem", None, "tile", None),
            P("mem", None, "tile", None),
            P("mem"),
            P("mem"),
            P("tile", None),
            P(("tile", "mem"), None),
            P(("tile", "mem")),
            P(("tile", "mem")),
            P(("tile", "mem")),
            P(None, ("tile", "mem")),
            P(("tile", "mem")),
            P(("tile", "mem")),
        ),
        out_specs=(P("mem", None, "tile", None), P(("tile", "mem"))),
        check_vma=False,
    )
```

```python
import functools

import jax
import jax.numpy as jnp
from jax import lax
from jax.experimental import pallas as pl
from jax.experimental.pallas import tpu as pltpu
from jax.sharding import PartitionSpec as P

STEPS = 8
COMPS = 8
LANES = 128
HIGHEST = lax.Precision.HIGHEST
F32 = jnp.float32
BF16 = jnp.bfloat16
COPY_FLOPS = 0
PARTIAL_FLOPS = 10**11


def iota(shape, dim):
    return lax.broadcasted_iota(jnp.int32, shape, dim)


def call(body, out_shape, in_specs=None, scratch=(), flops=0, moved=0, name=None):
    return pl.pallas_call(
        body,
        out_shape=out_shape,
        in_specs=in_specs,
        scratch_shapes=scratch,
        compiler_params=pltpu.CompilerParams(vmem_limit_bytes=48 * 2**20),
        cost_estimate=pl.CostEstimate(flops=flops, bytes_accessed=moved, transcendentals=0),
        name=name,
    )


VMEM = pl.BlockSpec(memory_space=pltpu.VMEM)
SMEM = pl.BlockSpec(memory_space=pltpu.SMEM)
ANY = pl.BlockSpec(memory_space=pl.ANY)


def vmem(count):
    return [VMEM] * count


def ranks(tile_row):
    count = tile_row.shape[1]
    along = jnp.broadcast_to(tile_row, (count, count))
    down = along.T
    i, j = iota((count, count), 0), iota((count, count), 1)
    same = along == down
    column = jnp.sum(jnp.where(same & (j < i), 1.0, 0.0), axis=1, keepdims=True)
    row = jnp.sum(jnp.where(same & (i < j), 1.0, 0.0), axis=0, keepdims=True)
    return column, row


def pack_body(
    tiles, slots, levels, tile_ref, row_ref, col_ref, lev_ref, weights_ref, value_ref, rinv_ref, send_ref, data_ref
):
    tile_row = tile_ref[...].astype(F32)
    data_ref[0:1, :] = col_ref[...].astype(F32)
    data_ref[1:2, :] = (row_ref[...] * levels + lev_ref[...]).astype(F32)
    data_ref[2:6, :] = weights_ref[...]
    data_ref[6:7, :] = value_ref[...]
    data_ref[7:8, :] = rinv_ref[...]
    count = tile_row.shape[1]
    column, unused = ranks(tile_row)
    width = COMPS * slots
    expand = jnp.where(iota((COMPS, width), 1) // slots == iota((COMPS, width), 0), 1.0, 0.0)
    data = lax.dot_general(
        data_ref[...], expand, (((0,), (0,)), ((), ())), precision=HIGHEST, preferred_element_type=F32
    )
    slot = (iota((count, width), 1) % slots).astype(F32)
    data = jnp.where(column == slot, data, 0.0)
    choose = jnp.where(iota((tiles, count), 0).astype(F32) == tile_row, 1.0, 0.0)
    send_ref[...] = jnp.dot(choose, data, precision=HIGHEST, preferred_element_type=F32)


def unpack_body(tile_ref, back_ref, hofx_ref):
    tile_row = tile_ref[...].astype(F32)
    tiles, slots = back_ref.shape
    count = tile_row.shape[1]
    unused, row = ranks(tile_row)
    choose = jnp.where(iota((tiles, count), 0).astype(F32) == tile_row, 1.0, 0.0)
    found = lax.dot_general(
        back_ref[...], choose, (((0,), (0,)), ((), ())), precision=HIGHEST, preferred_element_type=F32
    )
    keep = iota((slots, count), 0).astype(F32) == row
    hofx_ref[...] = jnp.sum(jnp.where(keep, found, 0.0), axis=0, keepdims=True)


def rates(group, keep, rate_x_ref, rate_y_ref):
    first = iota((8, LANES), 0) < 4
    rx = jnp.where(first, rate_x_ref[2 * group], rate_x_ref[2 * group + 1])
    ry = jnp.where(first, rate_y_ref[2 * group], rate_y_ref[2 * group + 1])
    centre = 1.0 - 2.0 * rx - 2.0 * ry
    return [(centre * k, rx * k, ry * k) for k in keep]


def smooth_rows(work, rows, coefs, emit):
    total = rows + 2 * STEPS
    parts = work.shape[2] // LANES
    lane = iota((8, LANES), 1)
    at_left, at_right = lane == 0, lane == LANES - 1

    def load(r):
        return [work[r, :, j * LANES : (j + 1) * LANES] for j in range(parts)]

    for step in range(STEPS):
        before, here = load(step), load(step + 1)
        for r in range(step + 1, total - 1 - step):
            after = load(r + 1)
            centre, rx, ry = coefs[0 if r < STEPS else (2 if r >= STEPS + rows else 1)]
            right = [pltpu.roll(v, 1, 1) for v in here]
            left = [pltpu.roll(v, LANES - 1, 1) for v in here]
            new = []
            for j in range(parts):
                low = jnp.where(at_left, right[j - 1] if j > 0 else 0.0, right[j])
                high = jnp.where(at_right, left[j + 1] if j + 1 < parts else 0.0, left[j])
                new.append(centre * here[j] + rx * (low + high) + ry * (before[j] + after[j]))
            if step == STEPS - 1:
                emit(r - STEPS, new)
            else:
                for j in range(parts):
                    work[r, :, j * LANES : (j + 1) * LANES] = new[j]
            before, here = here, after


def tiled(x):
    columns = x.shape[-1]
    x = x.reshape(-1, 8, columns // LANES, LANES)
    return jnp.swapaxes(x, 1, 2).reshape(-1, LANES)


def untiled(x, shape):
    x = x.reshape(-1, shape[-1] // LANES, 8, LANES)
    return jnp.swapaxes(x, 1, 2).reshape(shape)


def at_fields(base, stride, group, r, j, parts):
    return pl.ds(base + group * 8 * stride + (r // 8 * parts + j) * 8 + r % 8, 8, stride=stride)


def odd_tile():
    return lax.rem(lax.axis_index("tile"), 2)


def keep_sides(tiles):
    place = lax.axis_index("tile")
    return jnp.where(place > 0, 1.0, 0.0), jnp.where(place < tiles - 1, 1.0, 0.0)


def prep_body(unused_ref, alpha_ref, members_ref, land_ref, own_ref, masked_ref, far_ref, far_members_ref, near_ref):
    members, levels, rows, columns = members_ref.shape
    parts = columns // LANES
    size = rows * parts
    count = members * levels
    land = land_ref[...].astype(F32)
    for f in range(count):
        field = land * members_ref[f // levels, f % levels].astype(F32)
        for k in range(rows // 8):
            for j in range(parts):
                at = f * size + (k * parts + j) * 8
                mask = land[k * 8 : k * 8 + 8, j * LANES : (j + 1) * LANES]
                own_ref[at : at + 8, :] = mask * alpha_ref[at : at + 8, :]
                masked_ref[at : at + 8, :] = field[k * 8 : k * 8 + 8, j * LANES : (j + 1) * LANES]
    brim = STEPS * parts
    odd = odd_tile()
    first = odd * (size - brim)
    last = (1 - odd) * (size - brim)
    for source, far, start in ((own_ref, far_ref, 0), (masked_ref, far_members_ref, count * brim)):
        for f in range(count):
            to = f * brim
            far[to : to + brim, :] = source[pl.ds(pl.multiple_of(f * size + first, 8), brim), :]
            to = start + f * brim
            near_ref[to : to + brim, :] = source[pl.ds(pl.multiple_of(f * size + last, 8), brim), :]


def partial_body(rows, tiles, rate_x_ref, rate_y_ref, own_ref, far_ref, near_ref, members_ref, out_ref, work):
    parts = out_ref.shape[1] // LANES
    size, brim = rows * parts, STEPS * parts
    odd = odd_tile()
    far_at, near_at = odd * (rows + STEPS), (1 - odd) * (rows + STEPS)
    below, above = keep_sides(tiles)
    for group in range(2):
        for j in range(parts):
            lanes = slice(j * LANES, (j + 1) * LANES)
            for r in range(STEPS):
                work[far_at + r, :, lanes] = far_ref[at_fields(0, brim, group, r, j, parts), :]
                work[near_at + r, :, lanes] = near_ref[at_fields(0, brim, group, r, j, parts), :]
            for r in range(rows):
                work[STEPS + r, :, lanes] = own_ref[at_fields(0, size, group, r, j, parts), :]
        coefs = rates(group, (below, 1.0, above), rate_x_ref, rate_y_ref)

        def emit(r, new, group=group):
            terms = [new[j] * members_ref[at_fields(0, size, group, r, j, parts), :] for j in range(parts)]
            if group == 0:
                for j in range(parts):
                    out_ref[r * 8 : r * 8 + 8, j * LANES : (j + 1) * LANES] = terms[j]
                return
            lane, half = iota((8, LANES), 1), iota((8, LANES), 0) < 4
            sums = []
            for j in range(parts):
                both = terms[j] + out_ref[r * 8 : r * 8 + 8, j * LANES : (j + 1) * LANES]
                sums.append(both + pltpu.roll(both, 4, 0))
            left = [pltpu.roll(v, LANES - 1, 1) for v in sums]
            for j in range(parts):
                later = left[j + 1] if j + 1 < parts else left[j]
                shifted = jnp.where(lane == LANES - 1, later, left[j])
                out_ref[r * 8 : r * 8 + 8, j * LANES : (j + 1) * LANES] = jnp.where(
                    half, sums[j], shifted
                )

        smooth_rows(work, rows, coefs, emit)


def grad_body(
    rows,
    tiles,
    factor,
    rate_x_ref,
    rate_y_ref,
    alpha_ref,
    land_ref,
    members_ref,
    far_ref,
    near_ref,
    adjoint_ref,
    adjoint_far_ref,
    adjoint_near_ref,
    out_ref,
    work,
):
    parts = land_ref.shape[1] // LANES
    size, brim = rows * parts, STEPS * parts
    odd = odd_tile()
    far_at, near_at = odd * (rows + STEPS), (1 - odd) * (rows + STEPS)
    below, above = keep_sides(tiles)

    def twice(ref, r, lanes):
        four = ref[r * 4 : r * 4 + 4, lanes]
        return jnp.concatenate([four, four], axis=0)

    for group in range(2):
        for j in range(parts):
            lanes = slice(j * LANES, (j + 1) * LANES)
            for r in range(STEPS):
                at = at_fields(0, brim, group, r, j, parts)
                work[far_at + r, :, lanes] = far_ref[at, :] * twice(adjoint_far_ref, r, lanes)
                at = at_fields(16 * brim, brim, group, r, j, parts)
                work[near_at + r, :, lanes] = near_ref[at, :] * twice(adjoint_near_ref, r, lanes)
            for r in range(rows):
                own = members_ref[at_fields(0, size, group, r, j, parts), :]
                work[STEPS + r, :, lanes] = own * adjoint_ref[r * 8 : r * 8 + 8, lanes]
        coefs = rates(group, (below, 1.0, above), rate_x_ref, rate_y_ref)

        def emit(r, new, group=group):
            for j in range(parts):
                lanes = slice(j * LANES, (j + 1) * LANES)
                land = jnp.broadcast_to(land_ref[r : r + 1, lanes].astype(F32), (8, LANES)) * factor
                at = at_fields(0, size, group, r, j, parts)
                out_ref[at, :] = alpha_ref[at, :] + land * new[j]

        smooth_rows(work, rows, coefs, emit)


def corner_terms(s, slots, comps, scale):
    def comp(k):
        return comps[k * slots + s : k * slots + s + 1, :]

    count = comps.shape[1]
    code = comp(1)
    level = code - 4.0 * jnp.floor(code * 0.25)
    row = jnp.floor(code * 0.25)
    sub = iota((8, count), 0).astype(F32)
    weights = [comp(2 + k) if scale is None else comp(2 + k) * scale for k in range(4)]
    left, right = sub == level, sub == level + 4.0
    lower = jnp.where(left, weights[0], jnp.where(right, weights[1], 0.0))
    upper = jnp.where(left, weights[2], jnp.where(right, weights[3], 0.0))
    return jnp.broadcast_to(row, (8, count)), lower, upper


def interpolate_body(rows, slots, unused_ref, raw_ref, field_ref, comps_ref, out_ref, pieces, values):
    comps_ref[...] = raw_ref[...].T
    columns = field_ref.shape[1]
    count = comps_ref.shape[1]
    field = field_ref[...]
    top = field.astype(BF16)
    pieces[: 8 * rows, :] = top
    pieces[8 * rows :, :] = (field - top.astype(F32)).astype(BF16)
    for s in range(slots):
        column = comps_ref[s : s + 1, :].astype(jnp.int32)
        hot = jnp.where(iota((columns, count), 0) == column, 1.0, 0.0).astype(BF16)
        found = jnp.dot(pieces[...], hot, preferred_element_type=F32)
        row, lower, upper = corner_terms(s, slots, comps_ref, None)
        total = jnp.zeros((8, count), F32)
        previous = None
        for g in range(rows):
            at = row == float(g)
            value = found[g * 8 : g * 8 + 8] + found[8 * (rows + g) : 8 * (rows + g) + 8]
            rest = 0.0 if previous is None else jnp.where(previous, upper, 0.0)
            total = total + jnp.where(at, lower, rest) * value
            previous = at
        values[s : s + 1, :] = jnp.sum(total, axis=0, keepdims=True)
    for k in range(out_ref.shape[0]):
        out_ref[k] = values[...]


def copies_body(unused_ref, in_ref, out_ref):
    for k in range(out_ref.shape[0]):
        out_ref[k] = in_ref[...]


def spread_body(
    rows, slots, tiles, factor, raw_ref, comps_ref, sums_ref, own_ref, far_ref, near_ref, back_ref, left, total
):
    columns = own_ref.shape[1]
    count = comps_ref.shape[1]
    hofx = sums_ref[0]
    for k in range(1, sums_ref.shape[0]):
        hofx = hofx + sums_ref[k]
    hofx = factor * hofx
    mine = iota((tiles, count), 1) == lax.axis_index("mem") * tiles + iota((tiles, count), 0)
    back_ref[...] = lax.dot_general(
        jnp.where(mine, 1.0, 0.0),
        hofx,
        (((1,), (1,)), ((), ())),
        precision=HIGHEST,
        preferred_element_type=F32,
    )
    value = comps_ref[6 * slots : 7 * slots, :]
    rinv = comps_ref[7 * slots : 8 * slots, :]
    dep = rinv * (hofx - value)
    for s in range(slots):
        row, lower, upper = corner_terms(s, slots, comps_ref, dep[s : s + 1, :])
        previous = None
        for g in range(rows):
            at = row == float(g)
            rest = 0.0 if previous is None else jnp.where(previous, upper, 0.0)
            term = jnp.where(at, lower, rest)
            top = term.astype(BF16)
            left[g * 8 : g * 8 + 8, :] = top
            left[8 * (rows + g) : 8 * (rows + g) + 8, :] = (term - top.astype(F32)).astype(BF16)
            previous = at
        column = raw_ref[:, s : s + 1].astype(jnp.int32)
        hot = jnp.where(iota((count, columns), 1) == column, 1.0, 0.0).astype(BF16)
        part = jnp.dot(left[...], hot, preferred_element_type=F32)
        if s == 0:
            total[...] = part
        else:
            total[...] += part
    lane, half = iota((8, columns), 1), iota((8, columns), 0) < 4
    for g in range(rows):
        both = total[g * 8 : g * 8 + 8, :] + total[8 * (rows + g) : 8 * (rows + g) + 8, :]
        moved = jnp.where(lane == 0, 0.0, pltpu.roll(pltpu.roll(both, 4, 0), 1, 1))
        four = both + moved
        own_ref[g * 8 : g * 8 + 8, :] = jnp.where(half, four, pltpu.roll(four, 4, 0))
    odd = odd_tile()
    first, last = odd * (rows - STEPS), (1 - odd) * (rows - STEPS)
    for ref, start in ((far_ref, first), (near_ref, last)):
        for r in range(STEPS):
            ref[r * 4 : r * 4 + 4, :] = own_ref[pl.ds(pl.multiple_of((start + r) * 8, 8), 8), :][:4]


def on_device(
    alpha,
    perturbs,
    diff_x,
    diff_y,
    land_mask,
    obs_tile,
    obs_row,
    obs_col,
    obs_lev,
    obs_weights,
    obs_value,
    obs_rinv,
):
    members, levels, rows, columns = alpha.shape
    tiles, mems = lax.axis_size("tile"), lax.axis_size("mem")
    factor = (mems * members - 1) ** (-0.5)
    slots = 16
    pairs = [(i, i + 1) for i in range(0, tiles - 1, 2)]
    near_pairs = pairs + [(b, a) for a, b in pairs]
    pairs = [(i, i + 1) for i in range(1, tiles - 1, 2)]
    far_pairs = pairs + [(b, a) for a, b in pairs]
    size = members * levels * rows * columns // LANES
    brim = members * levels * STEPS * columns // LANES

    def to_far(x):
        return lax.ppermute(x, "tile", far_pairs)

    def to_near(x):
        return lax.ppermute(x, "tile", near_pairs)

    count = obs_row.shape[0]
    tile_row = obs_tile.reshape(1, count)
    width = COMPS * slots
    sent = call(
        functools.partial(pack_body, tiles, slots, levels),
        jax.ShapeDtypeStruct((tiles, width), F32),
        vmem(7),
        [pltpu.VMEM((COMPS, count), F32)],
        name="pack",
    )(
        tile_row,
        obs_row.reshape(1, count),
        obs_col.reshape(1, count),
        obs_lev.reshape(1, count),
        obs_weights,
        obs_value.reshape(1, count),
        obs_rinv.reshape(1, count),
    )
    routed = lax.all_to_all(sent, "tile", split_axis=0, concat_axis=0, tiled=True)

    alpha_tiles = tiled(alpha)
    own, masked, far, far_members, near = call(
        prep_body,
        (
            jax.ShapeDtypeStruct((size, LANES), F32),
            jax.ShapeDtypeStruct((size, LANES), F32),
            jax.ShapeDtypeStruct((brim, LANES), F32),
            jax.ShapeDtypeStruct((brim, LANES), F32),
            jax.ShapeDtypeStruct((2 * brim, LANES), F32),
        ),
        [ANY] + vmem(3),
        name="prep",
    )(routed, alpha_tiles, perturbs, land_mask)
    halo_far, halo_near = to_far(far), to_near(near)

    copied = call(
        copies_body,
        jax.ShapeDtypeStruct((mems, tiles, width), F32),
        [ANY] + vmem(1),
        flops=COPY_FLOPS,
        name="copies",
    )(far, routed)
    count = mems * tiles
    raw = lax.all_to_all(copied, "mem", split_axis=0, concat_axis=0, tiled=True).reshape(count, width)
    members_far = to_far(far_members)

    work = pltpu.VMEM((rows + 2 * STEPS, 8, columns), F32)
    partial = call(
        functools.partial(partial_body, rows, tiles),
        jax.ShapeDtypeStruct((8 * rows, columns), F32),
        [SMEM] * 2 + vmem(4),
        [work],
        flops=PARTIAL_FLOPS,
        name="partial",
    )(diff_x, diff_y, own, halo_far, halo_near, masked)
    comps, found = call(
        functools.partial(interpolate_body, rows, slots),
        (
            jax.ShapeDtypeStruct((width, count), F32),
            jax.ShapeDtypeStruct((mems, slots, count), F32),
        ),
        [ANY] + vmem(2),
        [pltpu.VMEM((16 * rows, columns), BF16), pltpu.VMEM((slots, count), F32)],
        name="interpolate",
    )(members_far, raw, partial)
    sums = lax.all_to_all(found, "mem", split_axis=0, concat_axis=0, tiled=True)
    edge = jax.ShapeDtypeStruct((levels * STEPS, columns), F32)
    adjoint, edge_far, edge_near, back = call(
        functools.partial(spread_body, rows, slots, tiles, factor),
        (
            jax.ShapeDtypeStruct((8 * rows, columns), F32),
            edge,
            edge,
            jax.ShapeDtypeStruct((tiles, slots), F32),
        ),
        vmem(3),
        [pltpu.VMEM((16 * rows, count), BF16), pltpu.VMEM((16 * rows, columns), F32)],
        name="spread",
    )(raw, comps, sums)
    adjoint_far, adjoint_near = to_far(edge_far), to_near(edge_near)
    returned = lax.all_to_all(back, "tile", split_axis=0, concat_axis=0, tiled=True)

    grad = call(
        functools.partial(grad_body, rows, tiles, factor),
        jax.ShapeDtypeStruct((size, LANES), F32),
        [SMEM] * 2 + vmem(8),
        [work],
        name="grad",
    )(
        diff_x,
        diff_y,
        alpha_tiles,
        land_mask,
        masked,
        members_far,
        halo_near,
        adjoint,
        adjoint_far,
        adjoint_near,
    )
    hofx = call(
        unpack_body,
        jax.ShapeDtypeStruct((1, obs_row.shape[0]), F32),
        vmem(2),
        name="unpack",
    )(tile_row, returned)
    return untiled(grad, alpha.shape), hofx.reshape(-1)


def solution(mesh):
    return jax.shard_map(
        on_device,
        mesh=mesh,
        in_specs=(
            P("mem", None, "tile", None),
            P("mem", None, "tile", None),
            P("mem"),
            P("mem"),
            P("tile", None),
            P(("tile", "mem"), None),
            P(("tile", "mem")),
            P(("tile", "mem")),
            P(("tile", "mem")),
            P(None, ("tile", "mem")),
            P(("tile", "mem")),
            P(("tile", "mem")),
        ),
        out_specs=(P("mem", None, "tile", None), P(("tile", "mem"))),
        check_vma=False,
    )
```

```python
import functools
import math

import jax
import jax.numpy as jnp
from jax import lax
from jax.experimental import pallas as pl
from jax.experimental.pallas import tpu as pltpu
from jax.sharding import PartitionSpec as P

STEPS = 8
COMPS = 8
LANES = 128
HIGHEST = lax.Precision.HIGHEST
F32 = jnp.float32
BF16 = jnp.bfloat16
PACK_FLOPS = 10**11
PARTIAL_FLOPS = 10**11
GRAD_FLOPS = 10**11


def iota(shape, dim):
    return lax.broadcasted_iota(jnp.int32, shape, dim)


def call(body, out_shape, in_specs=None, scratch=(), flops=0, moved=0, name=None, mib=48):
    return pl.pallas_call(
        body,
        out_shape=out_shape,
        in_specs=in_specs,
        scratch_shapes=scratch,
        compiler_params=pltpu.CompilerParams(vmem_limit_bytes=mib * 2**20),
        cost_estimate=pl.CostEstimate(flops=flops, bytes_accessed=moved, transcendentals=0),
        name=name,
    )


VMEM = pl.BlockSpec(memory_space=pltpu.VMEM)
SMEM = pl.BlockSpec(memory_space=pltpu.SMEM)
ANY = pl.BlockSpec(memory_space=pl.ANY)


def vmem(count):
    return [VMEM] * count


def ranks(tile_row):
    count = tile_row.shape[1]
    along = jnp.broadcast_to(tile_row, (count, count))
    down = along.T
    i, j = iota((count, count), 0), iota((count, count), 1)
    same = along == down
    column = jnp.sum(jnp.where(same & (j < i), 1.0, 0.0), axis=1, keepdims=True)
    row = jnp.sum(jnp.where(same & (i < j), 1.0, 0.0), axis=0, keepdims=True)
    return column, row


def pack_body(
    tiles, slots, levels, unused_ref, tile_ref, row_ref, col_ref, lev_ref, weights_ref, value_ref, rinv_ref, send_ref, data_ref
):
    tile_row = tile_ref[...].astype(F32)
    data_ref[0:1, :] = col_ref[...].astype(F32)
    data_ref[1:2, :] = (row_ref[...] * levels + lev_ref[...]).astype(F32)
    data_ref[2:6, :] = weights_ref[...]
    data_ref[6:7, :] = value_ref[...]
    data_ref[7:8, :] = rinv_ref[...]
    count = tile_row.shape[1]
    column, unused = ranks(tile_row)
    width = COMPS * slots
    expand = jnp.where(iota((COMPS, width), 1) // slots == iota((COMPS, width), 0), 1.0, 0.0)
    data = lax.dot_general(
        data_ref[...], expand, (((0,), (0,)), ((), ())), precision=HIGHEST, preferred_element_type=F32
    )
    slot = (iota((count, width), 1) % slots).astype(F32)
    data = jnp.where(column == slot, data, 0.0)
    choose = jnp.where(iota((tiles, count), 0).astype(F32) == tile_row, 1.0, 0.0)
    send_ref[...] = jnp.dot(choose, data, precision=HIGHEST, preferred_element_type=F32)


def unpack_body(unused_ref, tile_ref, back_ref, hofx_ref):
    tile_row = tile_ref[...].astype(F32)
    tiles, slots = back_ref.shape
    count = tile_row.shape[1]
    unused, row = ranks(tile_row)
    choose = jnp.where(iota((tiles, count), 0).astype(F32) == tile_row, 1.0, 0.0)
    found = lax.dot_general(
        back_ref[...], choose, (((0,), (0,)), ((), ())), precision=HIGHEST, preferred_element_type=F32
    )
    keep = iota((slots, count), 0).astype(F32) == row
    hofx_ref[...] = jnp.sum(jnp.where(keep, found, 0.0), axis=0, keepdims=True)


def rates(group, keep, rate_x_ref, rate_y_ref):
    first = iota((8, LANES), 0) < 4
    rx = jnp.where(first, rate_x_ref[2 * group], rate_x_ref[2 * group + 1])
    ry = jnp.where(first, rate_y_ref[2 * group], rate_y_ref[2 * group + 1])
    centre = 1.0 - 2.0 * rx - 2.0 * ry
    return [(centre * k, rx * k, ry * k) for k in keep]


def smooth_rows(work, rows, coefs, emit):
    total = rows + 2 * STEPS
    parts = work.shape[2] // LANES
    lane = iota((8, LANES), 1)
    at_left, at_right = lane == 0, lane == LANES - 1

    def load(r):
        return [work[r, :, j * LANES : (j + 1) * LANES] for j in range(parts)]

    for step in range(STEPS):
        before, here = load(step), load(step + 1)
        for r in range(step + 1, total - 1 - step):
            after = load(r + 1)
            centre, rx, ry = coefs[0 if r < STEPS else (2 if r >= STEPS + rows else 1)]
            right = [pltpu.roll(v, 1, 1) for v in here]
            left = [pltpu.roll(v, LANES - 1, 1) for v in here]
            new = []
            for j in range(parts):
                low = jnp.where(at_left, right[j - 1] if j > 0 else 0.0, right[j])
                high = jnp.where(at_right, left[j + 1] if j + 1 < parts else 0.0, left[j])
                new.append(centre * here[j] + rx * (low + high) + ry * (before[j] + after[j]))
            if step == STEPS - 1:
                emit(r - STEPS, new)
            else:
                for j in range(parts):
                    work[r, :, j * LANES : (j + 1) * LANES] = new[j]
            before, here = here, after


def tiled(x):
    columns = x.shape[-1]
    x = x.reshape(-1, 8, columns // LANES, LANES)
    return jnp.swapaxes(x, 1, 2).reshape(-1, LANES)


def untiled(x, shape):
    x = x.reshape(-1, shape[-1] // LANES, 8, LANES)
    return jnp.swapaxes(x, 1, 2).reshape(shape)


def at_fields(base, stride, group, r, j, parts):
    return pl.ds(base + group * 8 * stride + (r // 8 * parts + j) * 8 + r % 8, 8, stride=stride)


def odd_tile():
    return lax.rem(lax.axis_index("tile"), 2)


def keep_sides(tiles):
    place = lax.axis_index("tile")
    return jnp.where(place > 0, 1.0, 0.0), jnp.where(place < tiles - 1, 1.0, 0.0)


def prep_body(
    alpha_in, members_in, land_in, own_ref, masked_ref, far_ref, near_ref, alpha_ref, members_ref, land_ref, sems
):
    copies = [
        pltpu.make_async_copy(source, target, sems.at[k])
        for k, (source, target) in enumerate(
            ((land_in, land_ref), (members_in, members_ref), (alpha_in, alpha_ref))
        )
    ]
    for copy in copies:
        copy.start()
    for copy in copies:
        copy.wait()
    members, levels, rows, columns = members_ref.shape
    parts = columns // LANES
    size = rows * parts
    count = members * levels
    land = land_ref[...].astype(F32)
    for f in range(count):
        field = land * members_ref[f // levels, f % levels].astype(F32)
        for k in range(rows // 8):
            for j in range(parts):
                at = f * size + (k * parts + j) * 8
                mask = land[k * 8 : k * 8 + 8, j * LANES : (j + 1) * LANES]
                own_ref[at : at + 8, :] = mask * alpha_ref[at : at + 8, :]
                masked_ref[at : at + 8, :] = field[k * 8 : k * 8 + 8, j * LANES : (j + 1) * LANES]
    brim = STEPS * parts
    odd = odd_tile()
    first = odd * (size - brim)
    last = (1 - odd) * (size - brim)
    for source, start in ((own_ref, 0), (masked_ref, count * brim)):
        for f in range(count):
            to = slice(start + f * brim, start + (f + 1) * brim)
            far_ref[to, :] = source[pl.ds(pl.multiple_of(f * size + first, 8), brim), :]
            near_ref[to, :] = source[pl.ds(pl.multiple_of(f * size + last, 8), brim), :]


def partial_body(rows, tiles, rate_x_ref, rate_y_ref, own_ref, far_ref, near_ref, members_ref, out_ref, work):
    parts = out_ref.shape[1] // LANES
    size, brim = rows * parts, STEPS * parts
    odd = odd_tile()
    far_at, near_at = odd * (rows + STEPS), (1 - odd) * (rows + STEPS)
    below, above = keep_sides(tiles)
    for group in range(2):
        for j in range(parts):
            lanes = slice(j * LANES, (j + 1) * LANES)
            for r in range(STEPS):
                work[far_at + r, :, lanes] = far_ref[at_fields(0, brim, group, r, j, parts), :]
                work[near_at + r, :, lanes] = near_ref[at_fields(0, brim, group, r, j, parts), :]
            for r in range(rows):
                work[STEPS + r, :, lanes] = own_ref[at_fields(0, size, group, r, j, parts), :]
        coefs = rates(group, (below, 1.0, above), rate_x_ref, rate_y_ref)

        def emit(r, new, group=group):
            terms = [new[j] * members_ref[at_fields(0, size, group, r, j, parts), :] for j in range(parts)]
            if group == 0:
                for j in range(parts):
                    out_ref[r * 8 : r * 8 + 8, j * LANES : (j + 1) * LANES] = terms[j]
                return
            lane, half = iota((8, LANES), 1), iota((8, LANES), 0) < 4
            sums = []
            for j in range(parts):
                both = terms[j] + out_ref[r * 8 : r * 8 + 8, j * LANES : (j + 1) * LANES]
                sums.append(both + pltpu.roll(both, 4, 0))
            left = [pltpu.roll(v, LANES - 1, 1) for v in sums]
            for j in range(parts):
                later = left[j + 1] if j + 1 < parts else left[j]
                shifted = jnp.where(lane == LANES - 1, later, left[j])
                out_ref[r * 8 : r * 8 + 8, j * LANES : (j + 1) * LANES] = jnp.where(
                    half, sums[j], shifted
                )

        smooth_rows(work, rows, coefs, emit)


def grad_body(
    rows,
    tiles,
    factor,
    rate_x_ref,
    rate_y_ref,
    alpha_ref,
    land_ref,
    members_ref,
    far_ref,
    near_ref,
    adjoint_ref,
    adjoint_far_ref,
    adjoint_near_ref,
    out_ref,
    token_ref,
    work,
):
    token_ref[...] = jnp.zeros_like(token_ref)
    parts = land_ref.shape[1] // LANES
    size, brim = rows * parts, STEPS * parts
    odd = odd_tile()
    far_at, near_at = odd * (rows + STEPS), (1 - odd) * (rows + STEPS)
    below, above = keep_sides(tiles)

    def twice(ref, r, lanes):
        four = ref[r * 4 : r * 4 + 4, lanes]
        return jnp.concatenate([four, four], axis=0)

    for group in range(2):
        for j in range(parts):
            lanes = slice(j * LANES, (j + 1) * LANES)
            for r in range(STEPS):
                at = at_fields(16 * brim, brim, group, r, j, parts)
                work[far_at + r, :, lanes] = far_ref[at, :] * twice(adjoint_far_ref, r, lanes)
                work[near_at + r, :, lanes] = near_ref[at, :] * twice(adjoint_near_ref, r, lanes)
            for r in range(rows):
                own = members_ref[at_fields(0, size, group, r, j, parts), :]
                work[STEPS + r, :, lanes] = own * adjoint_ref[r * 8 : r * 8 + 8, lanes]
        coefs = rates(group, (below, 1.0, above), rate_x_ref, rate_y_ref)

        def emit(r, new, group=group):
            for j in range(parts):
                lanes = slice(j * LANES, (j + 1) * LANES)
                land = jnp.broadcast_to(land_ref[r : r + 1, lanes].astype(F32), (8, LANES)) * factor
                at = at_fields(0, size, group, r, j, parts)
                out_ref[at, :] = alpha_ref[at, :] + land * new[j]

        smooth_rows(work, rows, coefs, emit)


def corner_terms(s, slots, comps, scale):
    def comp(k):
        return comps[k * slots + s : k * slots + s + 1, :]

    count = comps.shape[1]
    code = comp(1)
    level = code - 4.0 * jnp.floor(code * 0.25)
    row = jnp.floor(code * 0.25)
    sub = iota((8, count), 0).astype(F32)
    weights = [comp(2 + k) if scale is None else comp(2 + k) * scale for k in range(4)]
    left, right = sub == level, sub == level + 4.0
    lower = jnp.where(left, weights[0], jnp.where(right, weights[1], 0.0))
    upper = jnp.where(left, weights[2], jnp.where(right, weights[3], 0.0))
    return jnp.broadcast_to(row, (8, count)), lower, upper


def interpolate_body(rows, slots, raw_ref, field_ref, comps_ref, out_ref, pieces):
    comps_ref[...] = raw_ref[...].T
    columns = field_ref.shape[1]
    count = comps_ref.shape[1]
    field = field_ref[...]
    top = field.astype(BF16)
    pieces[: 8 * rows, :] = top
    pieces[8 * rows :, :] = (field - top.astype(F32)).astype(BF16)
    for s in range(slots):
        column = comps_ref[s : s + 1, :].astype(jnp.int32)
        hot = jnp.where(iota((columns, count), 0) == column, 1.0, 0.0).astype(BF16)
        found = jnp.dot(pieces[...], hot, preferred_element_type=F32)
        row, lower, upper = corner_terms(s, slots, comps_ref, None)
        total = jnp.zeros((8, count), F32)
        previous = None
        for g in range(rows):
            at = row == float(g)
            value = found[g * 8 : g * 8 + 8] + found[8 * (rows + g) : 8 * (rows + g) + 8]
            rest = 0.0 if previous is None else jnp.where(previous, upper, 0.0)
            total = total + jnp.where(at, lower, rest) * value
            previous = at
        total = jnp.sum(total, axis=0, keepdims=True)
        for k in range(out_ref.shape[0]):
            out_ref[k, s : s + 1, :] = total


def copies_body(unused_ref, in_ref, out_ref):
    for k in range(out_ref.shape[0]):
        out_ref[k] = in_ref[...]


def add_body(in_ref, out_ref):
    total = in_ref[0]
    for k in range(1, in_ref.shape[0]):
        total = total + in_ref[k]
    for k in range(out_ref.shape[0]):
        out_ref[k] = total


def spread_body(
    rows, slots, tiles, factor, raw_ref, comps_ref, sums_ref, own_ref, far_ref, near_ref, back_ref, left, total
):
    columns = own_ref.shape[1]
    count = comps_ref.shape[1]
    hofx = sums_ref[0]
    for k in range(1, sums_ref.shape[0]):
        hofx = hofx + sums_ref[k]
    hofx = factor * hofx
    mine = iota((tiles, count), 1) == lax.axis_index("mem") * tiles + iota((tiles, count), 0)
    back_ref[...] = lax.dot_general(
        jnp.where(mine, 1.0, 0.0),
        hofx,
        (((1,), (1,)), ((), ())),
        precision=HIGHEST,
        preferred_element_type=F32,
    )
    value = comps_ref[6 * slots : 7 * slots, :]
    rinv = comps_ref[7 * slots : 8 * slots, :]
    dep = rinv * (hofx - value)
    for s in range(slots):
        row, lower, upper = corner_terms(s, slots, comps_ref, dep[s : s + 1, :])
        previous = None
        for g in range(rows):
            at = row == float(g)
            rest = 0.0 if previous is None else jnp.where(previous, upper, 0.0)
            term = jnp.where(at, lower, rest)
            top = term.astype(BF16)
            left[g * 8 : g * 8 + 8, :] = top
            left[8 * (rows + g) : 8 * (rows + g) + 8, :] = (term - top.astype(F32)).astype(BF16)
            previous = at
        column = raw_ref[:, s : s + 1].astype(jnp.int32)
        hot = jnp.where(iota((count, columns), 1) == column, 1.0, 0.0).astype(BF16)
        part = jnp.dot(left[...], hot, preferred_element_type=F32)
        if s == 0:
            total[...] = part
        else:
            total[...] += part
    lane, half = iota((8, columns), 1), iota((8, columns), 0) < 4
    for g in range(rows):
        both = total[g * 8 : g * 8 + 8, :] + total[8 * (rows + g) : 8 * (rows + g) + 8, :]
        moved = jnp.where(lane == 0, 0.0, pltpu.roll(pltpu.roll(both, 4, 0), 1, 1))
        four = both + moved
        own_ref[g * 8 : g * 8 + 8, :] = jnp.where(half, four, pltpu.roll(four, 4, 0))
    odd = odd_tile()
    first, last = odd * (rows - STEPS), (1 - odd) * (rows - STEPS)
    for ref, start in ((far_ref, first), (near_ref, last)):
        for r in range(STEPS):
            ref[r * 4 : r * 4 + 4, :] = own_ref[pl.ds(pl.multiple_of((start + r) * 8, 8), 8), :][:4]


def on_device(
    alpha,
    perturbs,
    diff_x,
    diff_y,
    land_mask,
    obs_tile,
    obs_row,
    obs_col,
    obs_lev,
    obs_weights,
    obs_value,
    obs_rinv,
):
    members, levels, rows, columns = alpha.shape
    tiles, mems = lax.axis_size("tile"), lax.axis_size("mem")
    factor = (mems * members - 1) ** (-0.5)
    slots = 16
    inner = math.isqrt(mems)
    near_group = [[i * inner + j for j in range(inner)] for i in range(inner)]
    far_group = [[i * inner + j for i in range(inner)] for j in range(inner)]
    pairs = [(i, i + 1) for i in range(0, tiles - 1, 2)]
    near_pairs = pairs + [(b, a) for a, b in pairs]
    pairs = [(i, i + 1) for i in range(1, tiles - 1, 2)]
    far_pairs = pairs + [(b, a) for a, b in pairs]
    size = members * levels * rows * columns // LANES
    brim = members * levels * STEPS * columns // LANES

    def exchange(far, near):
        return lax.ppermute(far, "tile", far_pairs), lax.ppermute(near, "tile", near_pairs)

    alpha_tiles = tiled(alpha)
    own, masked, far, near = call(
        prep_body,
        (
            jax.ShapeDtypeStruct((size, LANES), F32),
            jax.ShapeDtypeStruct((size, LANES), F32),
            jax.ShapeDtypeStruct((2 * brim, LANES), F32),
            jax.ShapeDtypeStruct((2 * brim, LANES), F32),
        ),
        [pl.BlockSpec(memory_space=pltpu.HBM)] * 3,
        [
            pltpu.VMEM(alpha_tiles.shape, F32),
            pltpu.VMEM(perturbs.shape, perturbs.dtype),
            pltpu.VMEM(land_mask.shape, land_mask.dtype),
            pltpu.SemaphoreType.DMA((3,)),
        ],
        name="prep",
        mib=60,
    )(alpha_tiles, perturbs, land_mask)
    halo_far, halo_near = exchange(far, near)

    count = obs_row.shape[0]
    tile_row = obs_tile.reshape(1, count)
    width = COMPS * slots
    sent = call(
        functools.partial(pack_body, tiles, slots, levels),
        jax.ShapeDtypeStruct((tiles, width), F32),
        [ANY] + vmem(7),
        [pltpu.VMEM((COMPS, count), F32)],
        flops=PACK_FLOPS,
        name="pack",
    )(
        far,
        tile_row,
        obs_row.reshape(1, count),
        obs_col.reshape(1, count),
        obs_lev.reshape(1, count),
        obs_weights,
        obs_value.reshape(1, count),
        obs_rinv.reshape(1, count),
    )
    routed = lax.all_to_all(sent, "tile", split_axis=0, concat_axis=0, tiled=True)
    count = mems * tiles
    work = pltpu.VMEM((rows + 2 * STEPS, 8, columns), F32)
    partial = call(
        functools.partial(partial_body, rows, tiles),
        jax.ShapeDtypeStruct((8 * rows, columns), F32),
        [SMEM] * 2 + vmem(4),
        [work],
        flops=PARTIAL_FLOPS,
        name="partial",
    )(diff_x, diff_y, own, halo_far, halo_near, masked)
    copied = call(
        copies_body,
        jax.ShapeDtypeStruct((mems, tiles, width), F32),
        [ANY] + vmem(1),
        name="copies",
    )(partial, routed)
    raw = lax.all_to_all(copied, "mem", split_axis=0, concat_axis=0, tiled=True).reshape(count, width)
    copies = jax.ShapeDtypeStruct((inner, slots, count), F32)
    comps, found = call(
        functools.partial(interpolate_body, rows, slots),
        (jax.ShapeDtypeStruct((width, count), F32), copies),
        vmem(2),
        [pltpu.VMEM((16 * rows, columns), BF16)],
        name="interpolate",
    )(raw, partial)

    def gather(x, groups):
        return lax.all_to_all(x, "mem", split_axis=0, concat_axis=0, axis_index_groups=groups, tiled=True)

    sums = gather(call(add_body, copies, vmem(1), name="add")(gather(found, near_group)), far_group)
    edge = jax.ShapeDtypeStruct((levels * STEPS, columns), F32)
    adjoint, edge_far, edge_near, back = call(
        functools.partial(spread_body, rows, slots, tiles, factor),
        (
            jax.ShapeDtypeStruct((8 * rows, columns), F32),
            edge,
            edge,
            jax.ShapeDtypeStruct((tiles, slots), F32),
        ),
        vmem(3),
        [pltpu.VMEM((16 * rows, count), BF16), pltpu.VMEM((16 * rows, columns), F32)],
        name="spread",
    )(raw, comps, sums)
    adjoint_far, adjoint_near = exchange(edge_far, edge_near)
    returned = lax.all_to_all(back, "tile", split_axis=0, concat_axis=0, tiled=True)

    grad, token = call(
        functools.partial(grad_body, rows, tiles, factor),
        (jax.ShapeDtypeStruct((size, LANES), F32), jax.ShapeDtypeStruct((8, LANES), F32)),
        [SMEM] * 2 + vmem(8),
        [work],
        flops=GRAD_FLOPS,
        name="grad",
    )(
        diff_x,
        diff_y,
        alpha_tiles,
        land_mask,
        masked,
        halo_far,
        halo_near,
        adjoint,
        adjoint_far,
        adjoint_near,
    )
    hofx = call(
        unpack_body,
        jax.ShapeDtypeStruct((1, obs_row.shape[0]), F32),
        [ANY] + vmem(2),
        name="unpack",
    )(token, tile_row, returned)
    return untiled(grad, alpha.shape), hofx.reshape(-1)


def solution(mesh):
    return jax.shard_map(
        on_device,
        mesh=mesh,
        in_specs=(
            P("mem", None, "tile", None),
            P("mem", None, "tile", None),
            P("mem"),
            P("mem"),
            P("tile", None),
            P(("tile", "mem"), None),
            P(("tile", "mem")),
            P(("tile", "mem")),
            P(("tile", "mem")),
            P(None, ("tile", "mem")),
            P(("tile", "mem")),
            P(("tile", "mem")),
        ),
        out_specs=(P("mem", None, "tile", None), P(("tile", "mem"))),
        check_vma=False,
    )
```

```python
import functools
import math

import jax
import jax.numpy as jnp
from jax import lax
from jax.experimental import pallas as pl
from jax.experimental.pallas import tpu as pltpu
from jax.sharding import PartitionSpec as P

STEPS = 8
COMPS = 8
LANES = 128
HIGHEST = lax.Precision.HIGHEST
F32 = jnp.float32
BF16 = jnp.bfloat16
PACK_FLOPS = 10**11
PARTIAL_FLOPS = 10**11
GRAD_FLOPS = 10**11


def iota(shape, dim):
    return lax.broadcasted_iota(jnp.int32, shape, dim)


def call(body, out_shape, in_specs=None, scratch=(), flops=0, moved=0, name=None, mib=48):
    return pl.pallas_call(
        body,
        out_shape=out_shape,
        in_specs=in_specs,
        scratch_shapes=scratch,
        compiler_params=pltpu.CompilerParams(vmem_limit_bytes=mib * 2**20),
        cost_estimate=pl.CostEstimate(flops=flops, bytes_accessed=moved, transcendentals=0),
        name=name,
    )


VMEM = pl.BlockSpec(memory_space=pltpu.VMEM)
SMEM = pl.BlockSpec(memory_space=pltpu.SMEM)
ANY = pl.BlockSpec(memory_space=pl.ANY)


def vmem(count):
    return [VMEM] * count


def ranks(tile_row):
    count = tile_row.shape[1]
    along = jnp.broadcast_to(tile_row, (count, count))
    down = along.T
    i, j = iota((count, count), 0), iota((count, count), 1)
    same = along == down
    column = jnp.sum(jnp.where(same & (j < i), 1.0, 0.0), axis=1, keepdims=True)
    row = jnp.sum(jnp.where(same & (i < j), 1.0, 0.0), axis=0, keepdims=True)
    return column, row


def pack(tiles, slots, tile_row, data):
    count = tile_row.shape[1]
    column, unused = ranks(tile_row)
    width = COMPS * slots
    expand = jnp.where(iota((COMPS, width), 1) // slots == iota((COMPS, width), 0), 1.0, 0.0)
    data = lax.dot_general(
        data, expand, (((0,), (0,)), ((), ())), precision=HIGHEST, preferred_element_type=F32
    )
    slot = (iota((count, width), 1) % slots).astype(F32)
    data = jnp.where(column == slot, data, 0.0)
    choose = jnp.where(iota((tiles, count), 0).astype(F32) == tile_row, 1.0, 0.0)
    return jnp.dot(choose, data, precision=HIGHEST, preferred_element_type=F32)


def unpack_body(unused_ref, info_ref, back_ref, hofx_ref):
    tile_row = info_ref[0:1, :]
    row = info_ref[1:2, :]
    tiles, slots = back_ref.shape
    count = tile_row.shape[1]
    choose = jnp.where(iota((tiles, count), 0).astype(F32) == tile_row, 1.0, 0.0)
    found = lax.dot_general(
        back_ref[...], choose, (((0,), (0,)), ((), ())), precision=HIGHEST, preferred_element_type=F32
    )
    keep = iota((slots, count), 0).astype(F32) == row
    hofx_ref[...] = jnp.sum(jnp.where(keep, found, 0.0), axis=0, keepdims=True)


def rates(group, keep, rate_x_ref, rate_y_ref):
    first = iota((8, LANES), 0) < 4
    rx = jnp.where(first, rate_x_ref[2 * group], rate_x_ref[2 * group + 1])
    ry = jnp.where(first, rate_y_ref[2 * group], rate_y_ref[2 * group + 1])
    centre = 1.0 - 2.0 * rx - 2.0 * ry
    return [(centre * k, rx * k, ry * k) for k in keep]


def smooth_rows(work, rows, coefs, emit):
    total = rows + 2 * STEPS
    parts = work.shape[2] // LANES
    lane = iota((8, LANES), 1)
    at_left, at_right = lane == 0, lane == LANES - 1

    def load(r):
        return [work[r, :, j * LANES : (j + 1) * LANES] for j in range(parts)]

    for step in range(STEPS):
        before, here = load(step), load(step + 1)
        for r in range(step + 1, total - 1 - step):
            after = load(r + 1)
            centre, rx, ry = coefs[0 if r < STEPS else (2 if r >= STEPS + rows else 1)]
            right = [pltpu.roll(v, 1, 1) for v in here]
            left = [pltpu.roll(v, LANES - 1, 1) for v in here]
            new = []
            for j in range(parts):
                low = jnp.where(at_left, right[j - 1] if j > 0 else 0.0, right[j])
                high = jnp.where(at_right, left[j + 1] if j + 1 < parts else 0.0, left[j])
                new.append(centre * here[j] + rx * (low + high) + ry * (before[j] + after[j]))
            if step == STEPS - 1:
                emit(r - STEPS, new)
            else:
                for j in range(parts):
                    work[r, :, j * LANES : (j + 1) * LANES] = new[j]
            before, here = here, after


def tiled(x):
    columns = x.shape[-1]
    x = x.reshape(-1, 8, columns // LANES, LANES)
    return jnp.swapaxes(x, 1, 2).reshape(-1, LANES)


def untiled(x, shape):
    x = x.reshape(-1, shape[-1] // LANES, 8, LANES)
    return jnp.swapaxes(x, 1, 2).reshape(shape)


def at_fields(base, stride, group, r, j, parts):
    return pl.ds(base + group * 8 * stride + (r // 8 * parts + j) * 8 + r % 8, 8, stride=stride)


def odd_tile():
    return lax.rem(lax.axis_index("tile"), 2)


def keep_sides(tiles):
    place = lax.axis_index("tile")
    return jnp.where(place > 0, 1.0, 0.0), jnp.where(place < tiles - 1, 1.0, 0.0)


def prep_body(tiles, slots, levels, *refs):
    sources, (far_ref, near_ref, sent_ref), buffers, (data_ref, sems) = (
        refs[:10],
        refs[10:13],
        refs[13:23],
        refs[23:],
    )
    copies = [
        pltpu.make_async_copy(source, target, sems.at[k])
        for k, (source, target) in enumerate(zip(sources, buffers))
    ]
    for copy in copies:
        copy.start()
    for copy in copies:
        copy.wait()
    alpha_ref, members_ref, land_ref, tile_ref, row_ref, col_ref, lev_ref, weights_ref, value_ref, rinv_ref = buffers
    members, unused, rows, columns = members_ref.shape
    parts = columns // LANES
    size, brim = rows * parts, STEPS * parts
    odd = odd_tile()
    land = land_ref[...].astype(F32)
    is_odd = jnp.broadcast_to(odd, (STEPS, columns)) == 1
    land_first, land_last = land[:STEPS], land[rows - STEPS :]
    land_far, land_near = jnp.where(is_odd, land_last, land_first), jnp.where(is_odd, land_first, land_last)
    count = members * levels
    for f in range(count):
        field = members_ref[f // levels, f % levels].astype(F32)
        first, last = field[:STEPS], field[rows - STEPS :]
        for ref, mask, top, start in (
            (far_ref, land_far, jnp.where(is_odd, last, first), odd * (size - brim)),
            (near_ref, land_near, jnp.where(is_odd, first, last), (1 - odd) * (size - brim)),
        ):
            value = mask * top
            for j in range(parts):
                lanes = slice(j * LANES, (j + 1) * LANES)
                at = pl.multiple_of(f * size + start + j * 8, 8)
                ref[f * brim + j * 8 : f * brim + j * 8 + 8, :] = mask[:, lanes] * alpha_ref[pl.ds(at, 8), :]
                at = (count + f) * brim + j * 8
                ref[at : at + 8, :] = value[:, lanes]
    tile_row = tile_ref[...].astype(F32)
    data_ref[0:1, :] = col_ref[...].astype(F32)
    data_ref[1:2, :] = (row_ref[...] * levels + lev_ref[...]).astype(F32)
    data_ref[2:6, :] = weights_ref[...]
    data_ref[6:7, :] = value_ref[...]
    data_ref[7:8, :] = rinv_ref[...]
    sent_ref[...] = pack(tiles, slots, tile_row, data_ref[...])


def mask_body(unused_ref, tile_ref, alpha_ref, members_ref, land_ref, own_ref, masked_ref, info_ref):
    tile_row = tile_ref[...].astype(F32)
    unused, rank = ranks(tile_row)
    info_ref[0:1, :] = tile_row
    info_ref[1:2, :] = rank
    members, levels, rows, columns = members_ref.shape
    parts = columns // LANES
    size = rows * parts
    land = land_ref[...].astype(F32)
    for f in range(members * levels):
        field = land * members_ref[f // levels, f % levels].astype(F32)
        for k in range(rows // 8):
            for j in range(parts):
                at = f * size + (k * parts + j) * 8
                mask = land[k * 8 : k * 8 + 8, j * LANES : (j + 1) * LANES]
                own_ref[at : at + 8, :] = mask * alpha_ref[at : at + 8, :]
                masked_ref[at : at + 8, :] = field[k * 8 : k * 8 + 8, j * LANES : (j + 1) * LANES]


def pass_body(in_ref, out_ref):
    def run(sem):
        copy = pltpu.make_async_copy(in_ref, out_ref, sem)
        copy.start()
        copy.wait()

    pl.run_scoped(run, pltpu.SemaphoreType.DMA(()))


def partial_body(rows, tiles, rate_x_ref, rate_y_ref, own_ref, far_ref, near_ref, members_ref, out_ref, work):
    parts = out_ref.shape[1] // LANES
    size, brim = rows * parts, STEPS * parts
    odd = odd_tile()
    far_at, near_at = odd * (rows + STEPS), (1 - odd) * (rows + STEPS)
    below, above = keep_sides(tiles)
    for group in range(2):
        for j in range(parts):
            lanes = slice(j * LANES, (j + 1) * LANES)
            for r in range(STEPS):
                work[far_at + r, :, lanes] = far_ref[at_fields(0, brim, group, r, j, parts), :]
                work[near_at + r, :, lanes] = near_ref[at_fields(0, brim, group, r, j, parts), :]
            for r in range(rows):
                work[STEPS + r, :, lanes] = own_ref[at_fields(0, size, group, r, j, parts), :]
        coefs = rates(group, (below, 1.0, above), rate_x_ref, rate_y_ref)

        def emit(r, new, group=group):
            terms = [new[j] * members_ref[at_fields(0, size, group, r, j, parts), :] for j in range(parts)]
            if group == 0:
                for j in range(parts):
                    out_ref[r * 8 : r * 8 + 8, j * LANES : (j + 1) * LANES] = terms[j]
                return
            lane, half = iota((8, LANES), 1), iota((8, LANES), 0) < 4
            sums = []
            for j in range(parts):
                both = terms[j] + out_ref[r * 8 : r * 8 + 8, j * LANES : (j + 1) * LANES]
                sums.append(both + pltpu.roll(both, 4, 0))
            left = [pltpu.roll(v, LANES - 1, 1) for v in sums]
            for j in range(parts):
                later = left[j + 1] if j + 1 < parts else left[j]
                shifted = jnp.where(lane == LANES - 1, later, left[j])
                out_ref[r * 8 : r * 8 + 8, j * LANES : (j + 1) * LANES] = jnp.where(
                    half, sums[j], shifted
                )

        smooth_rows(work, rows, coefs, emit)


def grad_body(
    rows,
    tiles,
    factor,
    rate_x_ref,
    rate_y_ref,
    alpha_ref,
    land_ref,
    members_ref,
    far_ref,
    near_ref,
    adjoint_ref,
    adjoint_far_ref,
    adjoint_near_ref,
    out_ref,
    token_ref,
    work,
):
    token_ref[...] = jnp.zeros_like(token_ref)
    parts = land_ref.shape[1] // LANES
    size, brim = rows * parts, STEPS * parts
    odd = odd_tile()
    far_at, near_at = odd * (rows + STEPS), (1 - odd) * (rows + STEPS)
    below, above = keep_sides(tiles)

    def twice(ref, r, lanes):
        four = ref[r * 4 : r * 4 + 4, lanes]
        return jnp.concatenate([four, four], axis=0)

    for group in range(2):
        for j in range(parts):
            lanes = slice(j * LANES, (j + 1) * LANES)
            for r in range(STEPS):
                at = at_fields(16 * brim, brim, group, r, j, parts)
                work[far_at + r, :, lanes] = far_ref[at, :] * twice(adjoint_far_ref, r, lanes)
                work[near_at + r, :, lanes] = near_ref[at, :] * twice(adjoint_near_ref, r, lanes)
            for r in range(rows):
                own = members_ref[at_fields(0, size, group, r, j, parts), :]
                work[STEPS + r, :, lanes] = own * adjoint_ref[r * 8 : r * 8 + 8, lanes]
        coefs = rates(group, (below, 1.0, above), rate_x_ref, rate_y_ref)

        def emit(r, new, group=group):
            for j in range(parts):
                lanes = slice(j * LANES, (j + 1) * LANES)
                land = jnp.broadcast_to(land_ref[r : r + 1, lanes].astype(F32), (8, LANES)) * factor
                at = at_fields(0, size, group, r, j, parts)
                out_ref[at, :] = alpha_ref[at, :] + land * new[j]

        smooth_rows(work, rows, coefs, emit)


def corner_terms(s, slots, comps, scale):
    def comp(k):
        return comps[k * slots + s : k * slots + s + 1, :]

    count = comps.shape[1]
    code = comp(1)
    level = code - 4.0 * jnp.floor(code * 0.25)
    row = jnp.floor(code * 0.25)
    sub = iota((8, count), 0).astype(F32)
    weights = [comp(2 + k) if scale is None else comp(2 + k) * scale for k in range(4)]
    left, right = sub == level, sub == level + 4.0
    lower = jnp.where(left, weights[0], jnp.where(right, weights[1], 0.0))
    upper = jnp.where(left, weights[2], jnp.where(right, weights[3], 0.0))
    return jnp.broadcast_to(row, (8, count)), lower, upper


def interpolate_body(rows, slots, raw_ref, field_ref, comps_ref, out_ref, pieces):
    comps_ref[...] = raw_ref[...].T
    columns = field_ref.shape[1]
    count = comps_ref.shape[1]
    field = field_ref[...]
    top = field.astype(BF16)
    pieces[: 8 * rows, :] = top
    pieces[8 * rows :, :] = (field - top.astype(F32)).astype(BF16)
    for s in range(slots):
        column = comps_ref[s : s + 1, :].astype(jnp.int32)
        hot = jnp.where(iota((columns, count), 0) == column, 1.0, 0.0).astype(BF16)
        found = jnp.dot(pieces[...], hot, preferred_element_type=F32)
        row, lower, upper = corner_terms(s, slots, comps_ref, None)
        total = jnp.zeros((8, count), F32)
        previous = None
        for g in range(rows):
            at = row == float(g)
            value = found[g * 8 : g * 8 + 8] + found[8 * (rows + g) : 8 * (rows + g) + 8]
            rest = 0.0 if previous is None else jnp.where(previous, upper, 0.0)
            total = total + jnp.where(at, lower, rest) * value
            previous = at
        total = jnp.sum(total, axis=0, keepdims=True)
        for k in range(out_ref.shape[0]):
            out_ref[k, s : s + 1, :] = total


def copies_body(unused_ref, in_ref, out_ref):
    for k in range(out_ref.shape[0]):
        out_ref[k] = in_ref[...]


def add_body(in_ref, out_ref):
    total = in_ref[0]
    for k in range(1, in_ref.shape[0]):
        total = total + in_ref[k]
    for k in range(out_ref.shape[0]):
        out_ref[k] = total


def spread_body(
    rows, slots, tiles, factor, raw_ref, comps_ref, sums_ref, own_ref, far_ref, near_ref, back_ref, left, total
):
    columns = own_ref.shape[1]
    count = comps_ref.shape[1]
    hofx = sums_ref[0]
    for k in range(1, sums_ref.shape[0]):
        hofx = hofx + sums_ref[k]
    hofx = factor * hofx
    mine = iota((tiles, count), 1) == lax.axis_index("mem") * tiles + iota((tiles, count), 0)
    back_ref[...] = lax.dot_general(
        jnp.where(mine, 1.0, 0.0),
        hofx,
        (((1,), (1,)), ((), ())),
        precision=HIGHEST,
        preferred_element_type=F32,
    )
    value = comps_ref[6 * slots : 7 * slots, :]
    rinv = comps_ref[7 * slots : 8 * slots, :]
    dep = rinv * (hofx - value)
    for s in range(slots):
        row, lower, upper = corner_terms(s, slots, comps_ref, dep[s : s + 1, :])
        previous = None
        for g in range(rows):
            at = row == float(g)
            rest = 0.0 if previous is None else jnp.where(previous, upper, 0.0)
            term = jnp.where(at, lower, rest)
            top = term.astype(BF16)
            left[g * 8 : g * 8 + 8, :] = top
            left[8 * (rows + g) : 8 * (rows + g) + 8, :] = (term - top.astype(F32)).astype(BF16)
            previous = at
        column = raw_ref[:, s : s + 1].astype(jnp.int32)
        hot = jnp.where(iota((count, columns), 1) == column, 1.0, 0.0).astype(BF16)
        part = jnp.dot(left[...], hot, preferred_element_type=F32)
        if s == 0:
            total[...] = part
        else:
            total[...] += part
    lane, half = iota((8, columns), 1), iota((8, columns), 0) < 4
    for g in range(rows):
        both = total[g * 8 : g * 8 + 8, :] + total[8 * (rows + g) : 8 * (rows + g) + 8, :]
        moved = jnp.where(lane == 0, 0.0, pltpu.roll(pltpu.roll(both, 4, 0), 1, 1))
        four = both + moved
        own_ref[g * 8 : g * 8 + 8, :] = jnp.where(half, four, pltpu.roll(four, 4, 0))
    odd = odd_tile()
    first, last = odd * (rows - STEPS), (1 - odd) * (rows - STEPS)
    for ref, start in ((far_ref, first), (near_ref, last)):
        for r in range(STEPS):
            ref[r * 4 : r * 4 + 4, :] = own_ref[pl.ds(pl.multiple_of((start + r) * 8, 8), 8), :][:4]


def on_device(
    alpha,
    perturbs,
    diff_x,
    diff_y,
    land_mask,
    obs_tile,
    obs_row,
    obs_col,
    obs_lev,
    obs_weights,
    obs_value,
    obs_rinv,
):
    members, levels, rows, columns = alpha.shape
    tiles, mems = lax.axis_size("tile"), lax.axis_size("mem")
    factor = (mems * members - 1) ** (-0.5)
    slots = 16
    inner = math.isqrt(mems)
    near_group = [[i * inner + j for j in range(inner)] for i in range(inner)]
    far_group = [[i * inner + j for i in range(inner)] for j in range(inner)]
    pairs = [(i, i + 1) for i in range(0, tiles - 1, 2)]
    near_pairs = pairs + [(b, a) for a, b in pairs]
    pairs = [(i, i + 1) for i in range(1, tiles - 1, 2)]
    far_pairs = pairs + [(b, a) for a, b in pairs]
    size = members * levels * rows * columns // LANES
    brim = members * levels * STEPS * columns // LANES

    def to_far(x):
        return lax.ppermute(x, "tile", far_pairs)

    def to_near(x):
        return lax.ppermute(x, "tile", near_pairs)

    alpha_tiles = tiled(alpha)
    count = obs_row.shape[0]
    width = COMPS * slots
    sources = (
        alpha_tiles,
        perturbs,
        land_mask,
        obs_tile.reshape(1, count),
        obs_row.reshape(1, count),
        obs_col.reshape(1, count),
        obs_lev.reshape(1, count),
        obs_weights,
        obs_value.reshape(1, count),
        obs_rinv.reshape(1, count),
    )
    far, near, sent = call(
        functools.partial(prep_body, tiles, slots, levels),
        (
            jax.ShapeDtypeStruct((2 * brim, LANES), F32),
            jax.ShapeDtypeStruct((2 * brim, LANES), F32),
            jax.ShapeDtypeStruct((tiles, width), F32),
        ),
        [ANY] * len(sources),
        [pltpu.VMEM(x.shape, x.dtype) for x in sources]
        + [pltpu.VMEM((COMPS, count), F32), pltpu.SemaphoreType.DMA((len(sources),))],
        name="prep",
        mib=60,
    )(*sources)
    halo_far, halo_near = to_far(far), to_near(near)
    sent = call(
        pass_body, jax.ShapeDtypeStruct(sent.shape, F32), [ANY], flops=PACK_FLOPS, name="pass", mib=60
    )(sent)
    routed = lax.all_to_all(sent, "tile", split_axis=0, concat_axis=0, tiled=True)
    own, masked, info = call(
        mask_body,
        (
            jax.ShapeDtypeStruct((size, LANES), F32),
            jax.ShapeDtypeStruct((size, LANES), F32),
            jax.ShapeDtypeStruct((2, count), F32),
        ),
        [ANY] + vmem(4),
        name="mask",
    )(sent, sources[3], alpha_tiles, perturbs, land_mask)
    count = mems * tiles
    work = pltpu.VMEM((rows + 2 * STEPS, 8, columns), F32)
    partial = call(
        functools.partial(partial_body, rows, tiles),
        jax.ShapeDtypeStruct((8 * rows, columns), F32),
        [SMEM] * 2 + vmem(4),
        [work],
        flops=PARTIAL_FLOPS,
        name="partial",
    )(diff_x, diff_y, own, halo_far, halo_near, masked)
    copied = call(
        copies_body,
        jax.ShapeDtypeStruct((mems, tiles, width), F32),
        [ANY] + vmem(1),
        name="copies",
    )(partial, routed)
    raw = lax.all_to_all(copied, "mem", split_axis=0, concat_axis=0, tiled=True).reshape(count, width)
    copies = jax.ShapeDtypeStruct((inner, slots, count), F32)
    comps, found = call(
        functools.partial(interpolate_body, rows, slots),
        (jax.ShapeDtypeStruct((width, count), F32), copies),
        vmem(2),
        [pltpu.VMEM((16 * rows, columns), BF16)],
        name="interpolate",
    )(raw, partial)

    def gather(x, groups):
        return lax.all_to_all(x, "mem", split_axis=0, concat_axis=0, axis_index_groups=groups, tiled=True)

    sums = gather(call(add_body, copies, vmem(1), name="add")(gather(found, near_group)), far_group)
    edge = jax.ShapeDtypeStruct((levels * STEPS, columns), F32)
    adjoint, edge_far, edge_near, back = call(
        functools.partial(spread_body, rows, slots, tiles, factor),
        (
            jax.ShapeDtypeStruct((8 * rows, columns), F32),
            edge,
            edge,
            jax.ShapeDtypeStruct((tiles, slots), F32),
        ),
        vmem(3),
        [pltpu.VMEM((16 * rows, count), BF16), pltpu.VMEM((16 * rows, columns), F32)],
        name="spread",
    )(raw, comps, sums)
    adjoint_far = to_far(edge_far)
    adjoint_near = to_near(edge_near)
    returned = lax.all_to_all(back, "tile", split_axis=0, concat_axis=0, tiled=True)

    grad, token = call(
        functools.partial(grad_body, rows, tiles, factor),
        (jax.ShapeDtypeStruct((size, LANES), F32), jax.ShapeDtypeStruct((8, LANES), F32)),
        [SMEM] * 2 + vmem(8),
        [work],
        flops=GRAD_FLOPS,
        name="grad",
    )(
        diff_x,
        diff_y,
        alpha_tiles,
        land_mask,
        masked,
        halo_far,
        halo_near,
        adjoint,
        adjoint_far,
        adjoint_near,
    )
    hofx = call(
        unpack_body,
        jax.ShapeDtypeStruct((1, obs_row.shape[0]), F32),
        [ANY] + vmem(2),
        name="unpack",
    )(token, info, returned)
    return untiled(grad, alpha.shape), hofx.reshape(-1)


def solution(mesh):
    return jax.shard_map(
        on_device,
        mesh=mesh,
        in_specs=(
            P("mem", None, "tile", None),
            P("mem", None, "tile", None),
            P("mem"),
            P("mem"),
            P("tile", None),
            P(("tile", "mem"), None),
            P(("tile", "mem")),
            P(("tile", "mem")),
            P(("tile", "mem")),
            P(None, ("tile", "mem")),
            P(("tile", "mem")),
            P(("tile", "mem")),
        ),
        out_specs=(P("mem", None, "tile", None), P(("tile", "mem"))),
        check_vma=False,
    )
```

```python
import functools
import math

import jax
import jax.numpy as jnp
from jax import lax
from jax.experimental import pallas as pl
from jax.experimental.pallas import tpu as pltpu
from jax.sharding import PartitionSpec as P

STEPS = 8
COMPS = 8
LANES = 128
HIGHEST = lax.Precision.HIGHEST
F32 = jnp.float32
BF16 = jnp.bfloat16
PARTIAL_FLOPS = 10**11
GRAD_FLOPS = 10**11


def iota(shape, dim):
    return lax.broadcasted_iota(jnp.int32, shape, dim)


def call(body, out_shape, in_specs=None, scratch=(), flops=0, moved=0, name=None, mib=48):
    return pl.pallas_call(
        body,
        out_shape=out_shape,
        in_specs=in_specs,
        scratch_shapes=scratch,
        compiler_params=pltpu.CompilerParams(vmem_limit_bytes=mib * 2**20),
        cost_estimate=pl.CostEstimate(flops=flops, bytes_accessed=moved, transcendentals=0),
        name=name,
    )


VMEM = pl.BlockSpec(memory_space=pltpu.VMEM)
SMEM = pl.BlockSpec(memory_space=pltpu.SMEM)
ANY = pl.BlockSpec(memory_space=pl.ANY)


def vmem(count):
    return [VMEM] * count


def ranks(tile_row):
    count = tile_row.shape[1]
    along = jnp.broadcast_to(tile_row, (count, count))
    down = along.T
    i, j = iota((count, count), 0), iota((count, count), 1)
    same = along == down
    column = jnp.sum(jnp.where(same & (j < i), 1.0, 0.0), axis=1, keepdims=True)
    row = jnp.sum(jnp.where(same & (i < j), 1.0, 0.0), axis=0, keepdims=True)
    return column, row


def pack(tiles, slots, tile_row, data):
    count = tile_row.shape[1]
    column, unused = ranks(tile_row)
    width = COMPS * slots
    expand = jnp.where(iota((COMPS, width), 1) // slots == iota((COMPS, width), 0), 1.0, 0.0)
    data = lax.dot_general(
        data, expand, (((0,), (0,)), ((), ())), precision=HIGHEST, preferred_element_type=F32
    )
    slot = (iota((count, width), 1) % slots).astype(F32)
    data = jnp.where(column == slot, data, 0.0)
    choose = jnp.where(iota((tiles, count), 0).astype(F32) == tile_row, 1.0, 0.0)
    return jnp.dot(choose, data, precision=HIGHEST, preferred_element_type=F32)


def unpack_body(unused_ref, info_ref, back_ref, hofx_ref):
    tile_row = info_ref[0:1, :]
    row = info_ref[1:2, :]
    tiles, slots = back_ref.shape
    count = tile_row.shape[1]
    choose = jnp.where(iota((tiles, count), 0).astype(F32) == tile_row, 1.0, 0.0)
    found = lax.dot_general(
        back_ref[...], choose, (((0,), (0,)), ((), ())), precision=HIGHEST, preferred_element_type=F32
    )
    keep = iota((slots, count), 0).astype(F32) == row
    hofx_ref[...] = jnp.sum(jnp.where(keep, found, 0.0), axis=0, keepdims=True)


def rates(group, keep, rate_x_ref, rate_y_ref):
    first = iota((8, LANES), 0) < 4
    rx = jnp.where(first, rate_x_ref[2 * group], rate_x_ref[2 * group + 1])
    ry = jnp.where(first, rate_y_ref[2 * group], rate_y_ref[2 * group + 1])
    centre = 1.0 - 2.0 * rx - 2.0 * ry
    return [(centre * k, rx * k, ry * k) for k in keep]


def smooth_rows(work, rows, coefs, emit):
    total = rows + 2 * STEPS
    parts = work.shape[2] // LANES
    lane = iota((8, LANES), 1)
    at_left, at_right = lane == 0, lane == LANES - 1

    def load(r):
        return [work[r, :, j * LANES : (j + 1) * LANES] for j in range(parts)]

    for step in range(STEPS):
        before, here = load(step), load(step + 1)
        for r in range(step + 1, total - 1 - step):
            after = load(r + 1)
            centre, rx, ry = coefs[0 if r < STEPS else (2 if r >= STEPS + rows else 1)]
            right = [pltpu.roll(v, 1, 1) for v in here]
            left = [pltpu.roll(v, LANES - 1, 1) for v in here]
            new = []
            for j in range(parts):
                low = jnp.where(at_left, right[j - 1] if j > 0 else 0.0, right[j])
                high = jnp.where(at_right, left[j + 1] if j + 1 < parts else 0.0, left[j])
                new.append(centre * here[j] + rx * (low + high) + ry * (before[j] + after[j]))
            if step == STEPS - 1:
                emit(r - STEPS, new)
            else:
                for j in range(parts):
                    work[r, :, j * LANES : (j + 1) * LANES] = new[j]
            before, here = here, after


def tiled(x):
    columns = x.shape[-1]
    x = x.reshape(-1, 8, columns // LANES, LANES)
    return jnp.swapaxes(x, 1, 2).reshape(-1, LANES)


def untiled(x, shape):
    x = x.reshape(-1, shape[-1] // LANES, 8, LANES)
    return jnp.swapaxes(x, 1, 2).reshape(shape)


def at_fields(base, stride, group, r, j, parts):
    return pl.ds(base + group * 8 * stride + (r // 8 * parts + j) * 8 + r % 8, 8, stride=stride)


def odd_tile():
    return lax.rem(lax.axis_index("tile"), 2)


def keep_sides(tiles):
    place = lax.axis_index("tile")
    return jnp.where(place > 0, 1.0, 0.0), jnp.where(place < tiles - 1, 1.0, 0.0)


def prep_body(tiles, slots, levels, *refs):
    sources, (far_ref, far_members_ref, near_ref, sent_ref), buffers, (data_ref, sems) = (
        refs[:10],
        refs[10:14],
        refs[14:24],
        refs[24:],
    )
    copies = [
        pltpu.make_async_copy(source, target, sems.at[k])
        for k, (source, target) in enumerate(zip(sources, buffers))
    ]
    for copy in copies:
        copy.start()
    for copy in copies:
        copy.wait()
    alpha_ref, members_ref, land_ref, tile_ref, row_ref, col_ref, lev_ref, weights_ref, value_ref, rinv_ref = buffers
    members, unused, rows, columns = members_ref.shape
    parts = columns // LANES
    size, brim = rows * parts, STEPS * parts
    odd = odd_tile()
    land = land_ref[...].astype(F32)
    is_odd = jnp.broadcast_to(odd, (STEPS, columns)) == 1
    land_first, land_last = land[:STEPS], land[rows - STEPS :]
    land_far, land_near = jnp.where(is_odd, land_last, land_first), jnp.where(is_odd, land_first, land_last)
    count = members * levels
    for f in range(count):
        field = members_ref[f // levels, f % levels].astype(F32)
        first, last = field[:STEPS], field[rows - STEPS :]
        for ref, other, mask, top, start in (
            (far_ref, far_members_ref, land_far, jnp.where(is_odd, last, first), odd * (size - brim)),
            (near_ref, near_ref, land_near, jnp.where(is_odd, first, last), (1 - odd) * (size - brim)),
        ):
            value = mask * top
            for j in range(parts):
                lanes = slice(j * LANES, (j + 1) * LANES)
                at = pl.multiple_of(f * size + start + j * 8, 8)
                ref[f * brim + j * 8 : f * brim + j * 8 + 8, :] = mask[:, lanes] * alpha_ref[pl.ds(at, 8), :]
                at = (f if other is far_members_ref else count + f) * brim + j * 8
                other[at : at + 8, :] = value[:, lanes]
    tile_row = tile_ref[...].astype(F32)
    data_ref[0:1, :] = col_ref[...].astype(F32)
    data_ref[1:2, :] = (row_ref[...] * levels + lev_ref[...]).astype(F32)
    data_ref[2:6, :] = weights_ref[...]
    data_ref[6:7, :] = value_ref[...]
    data_ref[7:8, :] = rinv_ref[...]
    sent_ref[...] = pack(tiles, slots, tile_row, data_ref[...])


def mask_body(unused_ref, tile_ref, alpha_ref, members_ref, land_ref, own_ref, masked_ref, info_ref):
    tile_row = tile_ref[...].astype(F32)
    unused, rank = ranks(tile_row)
    info_ref[0:1, :] = tile_row
    info_ref[1:2, :] = rank
    members, levels, rows, columns = members_ref.shape
    parts = columns // LANES
    size = rows * parts
    land = land_ref[...].astype(F32)
    for f in range(members * levels):
        field = land * members_ref[f // levels, f % levels].astype(F32)
        for k in range(rows // 8):
            for j in range(parts):
                at = f * size + (k * parts + j) * 8
                mask = land[k * 8 : k * 8 + 8, j * LANES : (j + 1) * LANES]
                own_ref[at : at + 8, :] = mask * alpha_ref[at : at + 8, :]
                masked_ref[at : at + 8, :] = field[k * 8 : k * 8 + 8, j * LANES : (j + 1) * LANES]


def partial_body(rows, tiles, rate_x_ref, rate_y_ref, own_ref, far_ref, near_ref, members_ref, out_ref, work):
    parts = out_ref.shape[1] // LANES
    size, brim = rows * parts, STEPS * parts
    odd = odd_tile()
    far_at, near_at = odd * (rows + STEPS), (1 - odd) * (rows + STEPS)
    below, above = keep_sides(tiles)
    for group in range(2):
        for j in range(parts):
            lanes = slice(j * LANES, (j + 1) * LANES)
            for r in range(STEPS):
                work[far_at + r, :, lanes] = far_ref[at_fields(0, brim, group, r, j, parts), :]
                work[near_at + r, :, lanes] = near_ref[at_fields(0, brim, group, r, j, parts), :]
            for r in range(rows):
                work[STEPS + r, :, lanes] = own_ref[at_fields(0, size, group, r, j, parts), :]
        coefs = rates(group, (below, 1.0, above), rate_x_ref, rate_y_ref)

        def emit(r, new, group=group):
            terms = [new[j] * members_ref[at_fields(0, size, group, r, j, parts), :] for j in range(parts)]
            if group == 0:
                for j in range(parts):
                    out_ref[r * 8 : r * 8 + 8, j * LANES : (j + 1) * LANES] = terms[j]
                return
            lane, half = iota((8, LANES), 1), iota((8, LANES), 0) < 4
            sums = []
            for j in range(parts):
                both = terms[j] + out_ref[r * 8 : r * 8 + 8, j * LANES : (j + 1) * LANES]
                sums.append(both + pltpu.roll(both, 4, 0))
            left = [pltpu.roll(v, LANES - 1, 1) for v in sums]
            for j in range(parts):
                later = left[j + 1] if j + 1 < parts else left[j]
                shifted = jnp.where(lane == LANES - 1, later, left[j])
                out_ref[r * 8 : r * 8 + 8, j * LANES : (j + 1) * LANES] = jnp.where(
                    half, sums[j], shifted
                )

        smooth_rows(work, rows, coefs, emit)


def grad_body(
    rows,
    tiles,
    factor,
    rate_x_ref,
    rate_y_ref,
    alpha_ref,
    land_ref,
    members_ref,
    far_ref,
    near_ref,
    adjoint_ref,
    adjoint_far_ref,
    adjoint_near_ref,
    out_ref,
    token_ref,
    work,
):
    token_ref[...] = jnp.zeros_like(token_ref)
    parts = land_ref.shape[1] // LANES
    size, brim = rows * parts, STEPS * parts
    odd = odd_tile()
    far_at, near_at = odd * (rows + STEPS), (1 - odd) * (rows + STEPS)
    below, above = keep_sides(tiles)

    def twice(ref, r, lanes):
        four = ref[r * 4 : r * 4 + 4, lanes]
        return jnp.concatenate([four, four], axis=0)

    for group in range(2):
        for j in range(parts):
            lanes = slice(j * LANES, (j + 1) * LANES)
            for r in range(STEPS):
                at = at_fields(0, brim, group, r, j, parts)
                work[far_at + r, :, lanes] = far_ref[at, :] * twice(adjoint_far_ref, r, lanes)
                at = at_fields(16 * brim, brim, group, r, j, parts)
                work[near_at + r, :, lanes] = near_ref[at, :] * twice(adjoint_near_ref, r, lanes)
            for r in range(rows):
                own = members_ref[at_fields(0, size, group, r, j, parts), :]
                work[STEPS + r, :, lanes] = own * adjoint_ref[r * 8 : r * 8 + 8, lanes]
        coefs = rates(group, (below, 1.0, above), rate_x_ref, rate_y_ref)

        def emit(r, new, group=group):
            for j in range(parts):
                lanes = slice(j * LANES, (j + 1) * LANES)
                land = jnp.broadcast_to(land_ref[r : r + 1, lanes].astype(F32), (8, LANES)) * factor
                at = at_fields(0, size, group, r, j, parts)
                out_ref[at, :] = alpha_ref[at, :] + land * new[j]

        smooth_rows(work, rows, coefs, emit)


def corner_terms(s, slots, comps, scale):
    def comp(k):
        return comps[k * slots + s : k * slots + s + 1, :]

    count = comps.shape[1]
    code = comp(1)
    level = code - 4.0 * jnp.floor(code * 0.25)
    row = jnp.floor(code * 0.25)
    sub = iota((8, count), 0).astype(F32)
    weights = [comp(2 + k) if scale is None else comp(2 + k) * scale for k in range(4)]
    left, right = sub == level, sub == level + 4.0
    lower = jnp.where(left, weights[0], jnp.where(right, weights[1], 0.0))
    upper = jnp.where(left, weights[2], jnp.where(right, weights[3], 0.0))
    return jnp.broadcast_to(row, (8, count)), lower, upper


def interpolate_body(rows, slots, raw_ref, field_ref, comps_ref, out_ref, pieces):
    comps_ref[...] = raw_ref[...].T
    columns = field_ref.shape[1]
    count = comps_ref.shape[1]
    field = field_ref[...]
    top = field.astype(BF16)
    pieces[: 8 * rows, :] = top
    pieces[8 * rows :, :] = (field - top.astype(F32)).astype(BF16)
    for s in range(slots):
        column = comps_ref[s : s + 1, :].astype(jnp.int32)
        hot = jnp.where(iota((columns, count), 0) == column, 1.0, 0.0).astype(BF16)
        found = jnp.dot(pieces[...], hot, preferred_element_type=F32)
        row, lower, upper = corner_terms(s, slots, comps_ref, None)
        total = jnp.zeros((8, count), F32)
        previous = None
        for g in range(rows):
            at = row == float(g)
            value = found[g * 8 : g * 8 + 8] + found[8 * (rows + g) : 8 * (rows + g) + 8]
            rest = 0.0 if previous is None else jnp.where(previous, upper, 0.0)
            total = total + jnp.where(at, lower, rest) * value
            previous = at
        total = jnp.sum(total, axis=0, keepdims=True)
        for k in range(out_ref.shape[0]):
            out_ref[k, s : s + 1, :] = total


def copies_body(unused_ref, in_ref, out_ref):
    for k in range(out_ref.shape[0]):
        out_ref[k] = in_ref[...]


def add_body(in_ref, out_ref):
    total = in_ref[0]
    for k in range(1, in_ref.shape[0]):
        total = total + in_ref[k]
    for k in range(out_ref.shape[0]):
        out_ref[k] = total


def spread_body(
    rows, slots, tiles, factor, raw_ref, comps_ref, sums_ref, own_ref, far_ref, near_ref, back_ref, left, total
):
    columns = own_ref.shape[1]
    count = comps_ref.shape[1]
    hofx = sums_ref[0]
    for k in range(1, sums_ref.shape[0]):
        hofx = hofx + sums_ref[k]
    hofx = factor * hofx
    mine = iota((tiles, count), 1) == lax.axis_index("mem") * tiles + iota((tiles, count), 0)
    back_ref[...] = lax.dot_general(
        jnp.where(mine, 1.0, 0.0),
        hofx,
        (((1,), (1,)), ((), ())),
        precision=HIGHEST,
        preferred_element_type=F32,
    )
    value = comps_ref[6 * slots : 7 * slots, :]
    rinv = comps_ref[7 * slots : 8 * slots, :]
    dep = rinv * (hofx - value)
    for s in range(slots):
        row, lower, upper = corner_terms(s, slots, comps_ref, dep[s : s + 1, :])
        previous = None
        for g in range(rows):
            at = row == float(g)
            rest = 0.0 if previous is None else jnp.where(previous, upper, 0.0)
            term = jnp.where(at, lower, rest)
            top = term.astype(BF16)
            left[g * 8 : g * 8 + 8, :] = top
            left[8 * (rows + g) : 8 * (rows + g) + 8, :] = (term - top.astype(F32)).astype(BF16)
            previous = at
        column = raw_ref[:, s : s + 1].astype(jnp.int32)
        hot = jnp.where(iota((count, columns), 1) == column, 1.0, 0.0).astype(BF16)
        part = jnp.dot(left[...], hot, preferred_element_type=F32)
        if s == 0:
            total[...] = part
        else:
            total[...] += part
    lane, half = iota((8, columns), 1), iota((8, columns), 0) < 4
    for g in range(rows):
        both = total[g * 8 : g * 8 + 8, :] + total[8 * (rows + g) : 8 * (rows + g) + 8, :]
        moved = jnp.where(lane == 0, 0.0, pltpu.roll(pltpu.roll(both, 4, 0), 1, 1))
        four = both + moved
        own_ref[g * 8 : g * 8 + 8, :] = jnp.where(half, four, pltpu.roll(four, 4, 0))
    odd = odd_tile()
    first, last = odd * (rows - STEPS), (1 - odd) * (rows - STEPS)
    for ref, start in ((far_ref, first), (near_ref, last)):
        for r in range(STEPS):
            ref[r * 4 : r * 4 + 4, :] = own_ref[pl.ds(pl.multiple_of((start + r) * 8, 8), 8), :][:4]


def on_device(
    alpha,
    perturbs,
    diff_x,
    diff_y,
    land_mask,
    obs_tile,
    obs_row,
    obs_col,
    obs_lev,
    obs_weights,
    obs_value,
    obs_rinv,
):
    members, levels, rows, columns = alpha.shape
    tiles, mems = lax.axis_size("tile"), lax.axis_size("mem")
    factor = (mems * members - 1) ** (-0.5)
    slots = 16
    inner = math.isqrt(mems)
    near_group = [[i * inner + j for j in range(inner)] for i in range(inner)]
    far_group = [[i * inner + j for i in range(inner)] for j in range(inner)]
    pairs = [(i, i + 1) for i in range(0, tiles - 1, 2)]
    near_pairs = pairs + [(b, a) for a, b in pairs]
    pairs = [(i, i + 1) for i in range(1, tiles - 1, 2)]
    far_pairs = pairs + [(b, a) for a, b in pairs]
    size = members * levels * rows * columns // LANES
    brim = members * levels * STEPS * columns // LANES

    def to_far(x):
        return lax.ppermute(x, "tile", far_pairs)

    def to_near(x):
        return lax.ppermute(x, "tile", near_pairs)

    alpha_tiles = tiled(alpha)
    count = obs_row.shape[0]
    width = COMPS * slots
    sources = (
        alpha_tiles,
        perturbs,
        land_mask,
        obs_tile.reshape(1, count),
        obs_row.reshape(1, count),
        obs_col.reshape(1, count),
        obs_lev.reshape(1, count),
        obs_weights,
        obs_value.reshape(1, count),
        obs_rinv.reshape(1, count),
    )
    far, far_members, near, sent = call(
        functools.partial(prep_body, tiles, slots, levels),
        (
            jax.ShapeDtypeStruct((brim, LANES), F32),
            jax.ShapeDtypeStruct((brim, LANES), F32),
            jax.ShapeDtypeStruct((2 * brim, LANES), F32),
            jax.ShapeDtypeStruct((tiles, width), F32),
        ),
        [ANY] * len(sources),
        [pltpu.VMEM(x.shape, x.dtype) for x in sources]
        + [pltpu.VMEM((COMPS, count), F32), pltpu.SemaphoreType.DMA((len(sources),))],
        name="prep",
        mib=60,
    )(*sources)
    halo_far, halo_near, members_far = to_far(far), to_near(near), to_far(far_members)
    routed = lax.all_to_all(sent, "tile", split_axis=0, concat_axis=0, tiled=True)
    own, masked, info = call(
        mask_body,
        (
            jax.ShapeDtypeStruct((size, LANES), F32),
            jax.ShapeDtypeStruct((size, LANES), F32),
            jax.ShapeDtypeStruct((2, count), F32),
        ),
        [ANY] + vmem(4),
        name="mask",
    )(sent, sources[3], alpha_tiles, perturbs, land_mask)
    count = mems * tiles
    work = pltpu.VMEM((rows + 2 * STEPS, 8, columns), F32)
    partial = call(
        functools.partial(partial_body, rows, tiles),
        jax.ShapeDtypeStruct((8 * rows, columns), F32),
        [SMEM] * 2 + vmem(4),
        [work],
        flops=PARTIAL_FLOPS,
        name="partial",
    )(diff_x, diff_y, own, halo_far, halo_near, masked)
    copied = call(
        copies_body,
        jax.ShapeDtypeStruct((mems, tiles, width), F32),
        [ANY] + vmem(1),
        name="copies",
    )(partial, routed)
    raw = lax.all_to_all(copied, "mem", split_axis=0, concat_axis=0, tiled=True).reshape(count, width)
    copies = jax.ShapeDtypeStruct((inner, slots, count), F32)
    comps, found = call(
        functools.partial(interpolate_body, rows, slots),
        (jax.ShapeDtypeStruct((width, count), F32), copies),
        vmem(2),
        [pltpu.VMEM((16 * rows, columns), BF16)],
        name="interpolate",
    )(raw, partial)

    def gather(x, groups):
        return lax.all_to_all(x, "mem", split_axis=0, concat_axis=0, axis_index_groups=groups, tiled=True)

    sums = gather(call(add_body, copies, vmem(1), name="add")(gather(found, near_group)), far_group)
    edge = jax.ShapeDtypeStruct((levels * STEPS, columns), F32)
    adjoint, edge_far, edge_near, back = call(
        functools.partial(spread_body, rows, slots, tiles, factor),
        (
            jax.ShapeDtypeStruct((8 * rows, columns), F32),
            edge,
            edge,
            jax.ShapeDtypeStruct((tiles, slots), F32),
        ),
        vmem(3),
        [pltpu.VMEM((16 * rows, count), BF16), pltpu.VMEM((16 * rows, columns), F32)],
        name="spread",
    )(raw, comps, sums)
    adjoint_far = to_far(edge_far)
    adjoint_near = to_near(edge_near)
    returned = lax.all_to_all(back, "tile", split_axis=0, concat_axis=0, tiled=True)

    grad, token = call(
        functools.partial(grad_body, rows, tiles, factor),
        (jax.ShapeDtypeStruct((size, LANES), F32), jax.ShapeDtypeStruct((8, LANES), F32)),
        [SMEM] * 2 + vmem(8),
        [work],
        flops=GRAD_FLOPS,
        name="grad",
    )(
        diff_x,
        diff_y,
        alpha_tiles,
        land_mask,
        masked,
        members_far,
        halo_near,
        adjoint,
        adjoint_far,
        adjoint_near,
    )
    hofx = call(
        unpack_body,
        jax.ShapeDtypeStruct((1, obs_row.shape[0]), F32),
        [ANY] + vmem(2),
        name="unpack",
    )(token, info, returned)
    return untiled(grad, alpha.shape), hofx.reshape(-1)


def solution(mesh):
    return jax.shard_map(
        on_device,
        mesh=mesh,
        in_specs=(
            P("mem", None, "tile", None),
            P("mem", None, "tile", None),
            P("mem"),
            P("mem"),
            P("tile", None),
            P(("tile", "mem"), None),
            P(("tile", "mem")),
            P(("tile", "mem")),
            P(("tile", "mem")),
            P(None, ("tile", "mem")),
            P(("tile", "mem")),
            P(("tile", "mem")),
        ),
        out_specs=(P("mem", None, "tile", None), P(("tile", "mem"))),
        check_vma=False,
    )
```

```python
import functools
import math

import jax
import jax.numpy as jnp
from jax import lax
from jax.experimental import pallas as pl
from jax.experimental.pallas import tpu as pltpu
from jax.sharding import PartitionSpec as P

STEPS = 8
COMPS = 8
LANES = 128
HIGHEST = lax.Precision.HIGHEST
F32 = jnp.float32
BF16 = jnp.bfloat16
I16 = jnp.int16
PARTIAL_FLOPS = 10**11
GRAD_FLOPS = 10**11


def iota(shape, dim):
    return lax.broadcasted_iota(jnp.int32, shape, dim)


def call(body, out_shape, in_specs=None, scratch=(), flops=0, moved=0, name=None, mib=48):
    return pl.pallas_call(
        body,
        out_shape=out_shape,
        in_specs=in_specs,
        scratch_shapes=scratch,
        compiler_params=pltpu.CompilerParams(vmem_limit_bytes=mib * 2**20),
        cost_estimate=pl.CostEstimate(flops=flops, bytes_accessed=moved, transcendentals=0),
        name=name,
    )


VMEM = pl.BlockSpec(memory_space=pltpu.VMEM)
SMEM = pl.BlockSpec(memory_space=pltpu.SMEM)
ANY = pl.BlockSpec(memory_space=pl.ANY)


def vmem(count):
    return [VMEM] * count


def ranks(tile_row):
    count = tile_row.shape[1]
    along = jnp.broadcast_to(tile_row, (count, count))
    down = along.T
    i, j = iota((count, count), 0), iota((count, count), 1)
    same = along == down
    column = jnp.sum(jnp.where(same & (j < i), 1.0, 0.0), axis=1, keepdims=True)
    row = jnp.sum(jnp.where(same & (i < j), 1.0, 0.0), axis=0, keepdims=True)
    return column, row


def pack(tiles, slots, tile_row, data):
    count = tile_row.shape[1]
    column, unused = ranks(tile_row)
    width = COMPS * slots
    expand = jnp.where(iota((COMPS, width), 1) // slots == iota((COMPS, width), 0), 1.0, 0.0)
    data = lax.dot_general(
        data, expand, (((0,), (0,)), ((), ())), precision=HIGHEST, preferred_element_type=F32
    )
    slot = (iota((count, width), 1) % slots).astype(F32)
    data = jnp.where(column == slot, data, 0.0)
    choose = jnp.where(iota((tiles, count), 0).astype(F32) == tile_row, 1.0, 0.0)
    return jnp.dot(choose, data, precision=HIGHEST, preferred_element_type=F32)


def unpack_body(unused_ref, info_ref, back_ref, hofx_ref):
    tile_row = info_ref[0:1, :]
    row = info_ref[1:2, :]
    tiles, slots = back_ref.shape
    count = tile_row.shape[1]
    choose = jnp.where(iota((tiles, count), 0).astype(F32) == tile_row, 1.0, 0.0)
    found = lax.dot_general(
        back_ref[...], choose, (((0,), (0,)), ((), ())), precision=HIGHEST, preferred_element_type=F32
    )
    keep = iota((slots, count), 0).astype(F32) == row
    hofx_ref[...] = jnp.sum(jnp.where(keep, found, 0.0), axis=0, keepdims=True)


def rates(group, keep, rate_x_ref, rate_y_ref):
    first = iota((8, LANES), 0) < 4
    rx = jnp.where(first, rate_x_ref[2 * group], rate_x_ref[2 * group + 1])
    ry = jnp.where(first, rate_y_ref[2 * group], rate_y_ref[2 * group + 1])
    centre = 1.0 - 2.0 * rx - 2.0 * ry
    return [(centre * k, rx * k, ry * k) for k in keep]


def smooth_rows(work, rows, coefs, emit):
    total = rows + 2 * STEPS
    parts = work.shape[2] // LANES
    lane = iota((8, LANES), 1)
    at_left, at_right = lane == 0, lane == LANES - 1

    def load(r):
        return [work[r, :, j * LANES : (j + 1) * LANES] for j in range(parts)]

    for step in range(STEPS):
        before, here = load(step), load(step + 1)
        for r in range(step + 1, total - 1 - step):
            after = load(r + 1)
            centre, rx, ry = coefs[0 if r < STEPS else (2 if r >= STEPS + rows else 1)]
            right = [pltpu.roll(v, 1, 1) for v in here]
            left = [pltpu.roll(v, LANES - 1, 1) for v in here]
            new = []
            for j in range(parts):
                low = jnp.where(at_left, right[j - 1] if j > 0 else 0.0, right[j])
                high = jnp.where(at_right, left[j + 1] if j + 1 < parts else 0.0, left[j])
                new.append(centre * here[j] + rx * (low + high) + ry * (before[j] + after[j]))
            if step == STEPS - 1:
                emit(r - STEPS, new)
            else:
                for j in range(parts):
                    work[r, :, j * LANES : (j + 1) * LANES] = new[j]
            before, here = here, after


def tiled(x):
    columns = x.shape[-1]
    x = x.reshape(-1, 8, columns // LANES, LANES)
    return jnp.swapaxes(x, 1, 2).reshape(-1, LANES)


def untiled(x, shape):
    x = x.reshape(-1, shape[-1] // LANES, 8, LANES)
    return jnp.swapaxes(x, 1, 2).reshape(shape)


def at_fields(base, stride, group, r, j, parts):
    return pl.ds(base + group * 8 * stride + (r // 8 * parts + j) * 8 + r % 8, 8, stride=stride)


def odd_tile():
    return lax.rem(lax.axis_index("tile"), 2)


def keep_sides(tiles):
    place = lax.axis_index("tile")
    return jnp.where(place > 0, 1.0, 0.0), jnp.where(place < tiles - 1, 1.0, 0.0)


def prep_body(tiles, slots, levels, *refs):
    sources, (far_ref, far_members_ref, near_ref, sent_ref), buffers, (data_ref, sems) = (
        refs[:10],
        refs[10:14],
        refs[14:24],
        refs[24:],
    )
    copies = [
        pltpu.make_async_copy(source, target, sems.at[k])
        for k, (source, target) in enumerate(zip(sources, buffers))
    ]
    for copy in copies:
        copy.start()
    for copy in copies:
        copy.wait()
    alpha_ref, members_ref, land_ref, tile_ref, row_ref, col_ref, lev_ref, weights_ref, value_ref, rinv_ref = buffers
    members, unused, rows, columns = members_ref.shape
    parts = columns // LANES
    size, brim = rows * parts, STEPS * parts
    odd = odd_tile()
    land = land_ref[...].astype(F32)
    is_odd = jnp.broadcast_to(odd, (STEPS, columns)) == 1
    land_first, land_last = land[:STEPS], land[rows - STEPS :]
    land_far, land_near = jnp.where(is_odd, land_last, land_first), jnp.where(is_odd, land_first, land_last)
    count = members * levels
    for f in range(count):
        field = members_ref[f // levels, f % levels].astype(F32)
        first, last = field[:STEPS], field[rows - STEPS :]
        for ref, other, mask, top, start in (
            (far_ref, far_members_ref, land_far, jnp.where(is_odd, last, first), odd * (size - brim)),
            (near_ref, near_ref, land_near, jnp.where(is_odd, first, last), (1 - odd) * (size - brim)),
        ):
            value = mask * top
            for j in range(parts):
                lanes = slice(j * LANES, (j + 1) * LANES)
                at = pl.multiple_of(f * size + start + j * 8, 8)
                ref[f * brim + j * 8 : f * brim + j * 8 + 8, :] = mask[:, lanes] * alpha_ref[pl.ds(at, 8), :]
                at = (f if other is far_members_ref else count + f) * brim + j * 8
                other[at : at + 8, :] = value[:, lanes]
    tile_row = tile_ref[...].astype(F32)
    data_ref[0:1, :] = col_ref[...].astype(F32)
    data_ref[1:2, :] = (row_ref[...] * levels + lev_ref[...]).astype(F32)
    data_ref[2:6, :] = weights_ref[...]
    data_ref[6:7, :] = value_ref[...]
    data_ref[7:8, :] = rinv_ref[...]
    sent_ref[...] = pack(tiles, slots, tile_row, data_ref[...])


def mask_body(unused_ref, tile_ref, alpha_ref, members_ref, land_ref, own_ref, masked_ref, info_ref):
    tile_row = tile_ref[...].astype(F32)
    unused, rank = ranks(tile_row)
    info_ref[0:1, :] = tile_row
    info_ref[1:2, :] = rank
    members, levels, rows, columns = members_ref.shape
    parts = columns // LANES
    size = rows * parts
    land = land_ref[...].astype(F32)
    for f in range(members * levels):
        field = land * members_ref[f // levels, f % levels].astype(F32)
        for k in range(rows // 8):
            for j in range(parts):
                at = f * size + (k * parts + j) * 8
                mask = land[k * 8 : k * 8 + 8, j * LANES : (j + 1) * LANES]
                own_ref[at : at + 8, :] = mask * alpha_ref[at : at + 8, :]
                masked_ref[at : at + 8, :] = field[k * 8 : k * 8 + 8, j * LANES : (j + 1) * LANES]


def partial_body(rows, tiles, rate_x_ref, rate_y_ref, own_ref, far_ref, near_ref, members_ref, out_ref, work):
    parts = out_ref.shape[1] // LANES
    size, brim = rows * parts, STEPS * parts
    odd = odd_tile()
    far_at, near_at = odd * (rows + STEPS), (1 - odd) * (rows + STEPS)
    below, above = keep_sides(tiles)
    for group in range(2):
        for j in range(parts):
            lanes = slice(j * LANES, (j + 1) * LANES)
            for r in range(STEPS):
                work[far_at + r, :, lanes] = far_ref[at_fields(0, brim, group, r, j, parts), :]
                work[near_at + r, :, lanes] = near_ref[at_fields(0, brim, group, r, j, parts), :]
            for r in range(rows):
                work[STEPS + r, :, lanes] = own_ref[at_fields(0, size, group, r, j, parts), :]
        coefs = rates(group, (below, 1.0, above), rate_x_ref, rate_y_ref)

        def emit(r, new, group=group):
            terms = [new[j] * members_ref[at_fields(0, size, group, r, j, parts), :] for j in range(parts)]
            if group == 0:
                for j in range(parts):
                    out_ref[r * 8 : r * 8 + 8, j * LANES : (j + 1) * LANES] = terms[j]
                return
            lane, half = iota((8, LANES), 1), iota((8, LANES), 0) < 4
            sums = []
            for j in range(parts):
                both = terms[j] + out_ref[r * 8 : r * 8 + 8, j * LANES : (j + 1) * LANES]
                sums.append(both + pltpu.roll(both, 4, 0))
            left = [pltpu.roll(v, LANES - 1, 1) for v in sums]
            for j in range(parts):
                later = left[j + 1] if j + 1 < parts else left[j]
                shifted = jnp.where(lane == LANES - 1, later, left[j])
                out_ref[r * 8 : r * 8 + 8, j * LANES : (j + 1) * LANES] = jnp.where(
                    half, sums[j], shifted
                )

        smooth_rows(work, rows, coefs, emit)


def grad_body(
    rows,
    tiles,
    factor,
    rate_x_ref,
    rate_y_ref,
    alpha_ref,
    land_ref,
    members_ref,
    far_ref,
    near_ref,
    adjoint_ref,
    adjoint_far_ref,
    adjoint_near_ref,
    out_ref,
    token_ref,
    work,
):
    token_ref[...] = jnp.zeros_like(token_ref)
    parts = land_ref.shape[1] // LANES
    size, brim = rows * parts, STEPS * parts
    odd = odd_tile()
    far_at, near_at = odd * (rows + STEPS), (1 - odd) * (rows + STEPS)
    below, above = keep_sides(tiles)

    def twice(ref, r, lanes):
        four = ref[r * 4 : r * 4 + 4, lanes]
        return jnp.concatenate([four, four], axis=0)

    for group in range(2):
        for j in range(parts):
            lanes = slice(j * LANES, (j + 1) * LANES)
            for r in range(STEPS):
                at = at_fields(0, brim, group, r, j, parts)
                work[far_at + r, :, lanes] = far_ref[at, :] * twice(adjoint_far_ref, r, lanes)
                at = at_fields(16 * brim, brim, group, r, j, parts)
                work[near_at + r, :, lanes] = near_ref[at, :] * twice(adjoint_near_ref, r, lanes)
            for r in range(rows):
                own = members_ref[at_fields(0, size, group, r, j, parts), :]
                work[STEPS + r, :, lanes] = own * adjoint_ref[r * 8 : r * 8 + 8, lanes]
        coefs = rates(group, (below, 1.0, above), rate_x_ref, rate_y_ref)

        def emit(r, new, group=group):
            for j in range(parts):
                lanes = slice(j * LANES, (j + 1) * LANES)
                land = jnp.broadcast_to(land_ref[r : r + 1, lanes].astype(F32), (8, LANES)) * factor
                at = at_fields(0, size, group, r, j, parts)
                out_ref[at, :] = alpha_ref[at, :] + land * new[j]

        smooth_rows(work, rows, coefs, emit)


def corner_terms(s, slots, comps, scale):
    def comp(k):
        return comps[k * slots + s : k * slots + s + 1, :]

    count = comps.shape[1]
    code = comp(1)
    level = code - 4.0 * jnp.floor(code * 0.25)
    row = jnp.floor(code * 0.25)
    sub = iota((8, count), 0).astype(F32)
    weights = [comp(2 + k) if scale is None else comp(2 + k) * scale for k in range(4)]
    left, right = sub == level, sub == level + 4.0
    lower = jnp.where(left, weights[0], jnp.where(right, weights[1], 0.0))
    upper = jnp.where(left, weights[2], jnp.where(right, weights[3], 0.0))
    return jnp.broadcast_to(row, (8, count)), lower, upper


def interpolate_body(rows, slots, raw_ref, field_ref, comps_ref, out_ref, pieces):
    comps_ref[...] = raw_ref[...].T
    columns = field_ref.shape[1]
    count = comps_ref.shape[1]
    field = field_ref[...]
    top = field.astype(BF16)
    pieces[: 8 * rows, :] = top
    pieces[8 * rows :, :] = (field - top.astype(F32)).astype(BF16)
    for s in range(slots):
        column = comps_ref[s : s + 1, :].astype(jnp.int32).astype(I16)
        hot = jnp.where(iota((columns, count), 0).astype(I16) == column, BF16(1.0), BF16(0.0))
        found = jnp.dot(pieces[...], hot, preferred_element_type=F32)
        row, lower, upper = corner_terms(s, slots, comps_ref, None)
        total = jnp.zeros((8, count), F32)
        previous = None
        for g in range(rows):
            at = row == float(g)
            value = found[g * 8 : g * 8 + 8] + found[8 * (rows + g) : 8 * (rows + g) + 8]
            rest = 0.0 if previous is None else jnp.where(previous, upper, 0.0)
            total = total + jnp.where(at, lower, rest) * value
            previous = at
        total = jnp.sum(total, axis=0, keepdims=True)
        for k in range(out_ref.shape[0]):
            out_ref[k, s : s + 1, :] = total


def copies_body(unused_ref, in_ref, out_ref):
    for k in range(out_ref.shape[0]):
        out_ref[k] = in_ref[...]


def add_body(in_ref, out_ref):
    total = in_ref[0]
    for k in range(1, in_ref.shape[0]):
        total = total + in_ref[k]
    for k in range(out_ref.shape[0]):
        out_ref[k] = total


def spread_scratch(rows, count, columns):
    return [
        pltpu.VMEM((16 * rows, count), BF16),
        pltpu.VMEM((count, columns), BF16),
        pltpu.VMEM((16 * rows, columns), F32),
    ]


def spread_body(
    rows, slots, tiles, factor, raw_ref, comps_ref, sums_ref, own_ref, far_ref, near_ref, back_ref, left, hot, total
):
    columns = own_ref.shape[1]
    count = comps_ref.shape[1]
    hofx = sums_ref[0]
    for k in range(1, sums_ref.shape[0]):
        hofx = hofx + sums_ref[k]
    hofx = factor * hofx
    mine = iota((tiles, count), 1) == lax.axis_index("mem") * tiles + iota((tiles, count), 0)
    back_ref[...] = lax.dot_general(
        jnp.where(mine, 1.0, 0.0),
        hofx,
        (((1,), (1,)), ((), ())),
        precision=HIGHEST,
        preferred_element_type=F32,
    )
    value = comps_ref[6 * slots : 7 * slots, :]
    rinv = comps_ref[7 * slots : 8 * slots, :]
    dep = rinv * (hofx - value)
    for s in range(slots):
        row, lower, upper = corner_terms(s, slots, comps_ref, dep[s : s + 1, :])
        previous, terms = None, []
        for g in range(rows):
            at = row == float(g)
            rest = 0.0 if previous is None else jnp.where(previous, upper, 0.0)
            terms.append(jnp.where(at, lower, rest))
            previous = at
            if g % 2 == 1:
                pair = jnp.concatenate(terms[-2:], axis=0)
                top = pair.astype(BF16)
                left[g * 8 - 8 : g * 8 + 8, :] = top
                left[8 * (rows + g) - 8 : 8 * (rows + g) + 8, :] = (pair - top.astype(F32)).astype(BF16)
        column = jnp.broadcast_to(raw_ref[:, s : s + 1].astype(jnp.int32), (count, LANES)).astype(I16)
        lane16 = iota((count, LANES), 1).astype(I16)
        for j in range(columns // LANES):
            lanes = slice(j * LANES, (j + 1) * LANES)
            hot[:, lanes] = jnp.where(lane16 + I16(j * LANES) == column, BF16(1.0), BF16(0.0))
        part = jnp.dot(left[...], hot[...], preferred_element_type=F32)
        if s == 0:
            total[...] = part
        else:
            total[...] += part
    lane, half = iota((8, columns), 1), iota((8, columns), 0) < 4
    for g in range(rows):
        both = total[g * 8 : g * 8 + 8, :] + total[8 * (rows + g) : 8 * (rows + g) + 8, :]
        moved = jnp.where(lane == 0, 0.0, pltpu.roll(pltpu.roll(both, 4, 0), 1, 1))
        four = both + moved
        own_ref[g * 8 : g * 8 + 8, :] = jnp.where(half, four, pltpu.roll(four, 4, 0))
    odd = odd_tile()
    first, last = odd * (rows - STEPS), (1 - odd) * (rows - STEPS)
    for ref, start in ((far_ref, first), (near_ref, last)):
        for r in range(STEPS):
            ref[r * 4 : r * 4 + 4, :] = own_ref[pl.ds(pl.multiple_of((start + r) * 8, 8), 8), :][:4]


def on_device(
    alpha,
    perturbs,
    diff_x,
    diff_y,
    land_mask,
    obs_tile,
    obs_row,
    obs_col,
    obs_lev,
    obs_weights,
    obs_value,
    obs_rinv,
):
    members, levels, rows, columns = alpha.shape
    tiles, mems = lax.axis_size("tile"), lax.axis_size("mem")
    factor = (mems * members - 1) ** (-0.5)
    slots = 16
    inner = math.isqrt(mems)
    near_group = [[i * inner + j for j in range(inner)] for i in range(inner)]
    far_group = [[i * inner + j for i in range(inner)] for j in range(inner)]
    pairs = [(i, i + 1) for i in range(0, tiles - 1, 2)]
    near_pairs = pairs + [(b, a) for a, b in pairs]
    pairs = [(i, i + 1) for i in range(1, tiles - 1, 2)]
    far_pairs = pairs + [(b, a) for a, b in pairs]
    size = members * levels * rows * columns // LANES
    brim = members * levels * STEPS * columns // LANES

    def to_far(x):
        return lax.ppermute(x, "tile", far_pairs)

    def to_near(x):
        return lax.ppermute(x, "tile", near_pairs)

    alpha_tiles = tiled(alpha)
    count = obs_row.shape[0]
    width = COMPS * slots
    sources = (
        alpha_tiles,
        perturbs,
        land_mask,
        obs_tile.reshape(1, count),
        obs_row.reshape(1, count),
        obs_col.reshape(1, count),
        obs_lev.reshape(1, count),
        obs_weights,
        obs_value.reshape(1, count),
        obs_rinv.reshape(1, count),
    )
    far, far_members, near, sent = call(
        functools.partial(prep_body, tiles, slots, levels),
        (
            jax.ShapeDtypeStruct((brim, LANES), F32),
            jax.ShapeDtypeStruct((brim, LANES), F32),
            jax.ShapeDtypeStruct((2 * brim, LANES), F32),
            jax.ShapeDtypeStruct((tiles, width), F32),
        ),
        [ANY] * len(sources),
        [pltpu.VMEM(x.shape, x.dtype) for x in sources]
        + [pltpu.VMEM((COMPS, count), F32), pltpu.SemaphoreType.DMA((len(sources),))],
        name="prep",
        mib=60,
    )(*sources)
    halo_far, halo_near, members_far = to_far(far), to_near(near), to_far(far_members)
    routed = lax.all_to_all(sent, "tile", split_axis=0, concat_axis=0, tiled=True)
    own, masked, info = call(
        mask_body,
        (
            jax.ShapeDtypeStruct((size, LANES), F32),
            jax.ShapeDtypeStruct((size, LANES), F32),
            jax.ShapeDtypeStruct((2, count), F32),
        ),
        [ANY] + vmem(4),
        name="mask",
    )(sent, sources[3], alpha_tiles, perturbs, land_mask)
    count = mems * tiles
    work = pltpu.VMEM((rows + 2 * STEPS, 8, columns), F32)
    partial = call(
        functools.partial(partial_body, rows, tiles),
        jax.ShapeDtypeStruct((8 * rows, columns), F32),
        [SMEM] * 2 + vmem(4),
        [work],
        flops=PARTIAL_FLOPS,
        name="partial",
    )(diff_x, diff_y, own, halo_far, halo_near, masked)
    copied = call(
        copies_body,
        jax.ShapeDtypeStruct((mems, tiles, width), F32),
        [ANY] + vmem(1),
        name="copies",
    )(partial, routed)
    raw = lax.all_to_all(copied, "mem", split_axis=0, concat_axis=0, tiled=True).reshape(count, width)
    copies = jax.ShapeDtypeStruct((inner, slots, count), F32)
    comps, found = call(
        functools.partial(interpolate_body, rows, slots),
        (jax.ShapeDtypeStruct((width, count), F32), copies),
        vmem(2),
        [pltpu.VMEM((16 * rows, columns), BF16)],
        name="interpolate",
    )(raw, partial)

    def gather(x, groups):
        return lax.all_to_all(x, "mem", split_axis=0, concat_axis=0, axis_index_groups=groups, tiled=True)

    sums = gather(call(add_body, copies, vmem(1), name="add")(gather(found, near_group)), far_group)
    edge = jax.ShapeDtypeStruct((levels * STEPS, columns), F32)
    adjoint, edge_far, edge_near, back = call(
        functools.partial(spread_body, rows, slots, tiles, factor),
        (
            jax.ShapeDtypeStruct((8 * rows, columns), F32),
            edge,
            edge,
            jax.ShapeDtypeStruct((tiles, slots), F32),
        ),
        vmem(3),
        spread_scratch(rows, count, columns),
        name="spread",
    )(raw, comps, sums)
    adjoint_far = to_far(edge_far)
    adjoint_near = to_near(edge_near)
    returned = lax.all_to_all(back, "tile", split_axis=0, concat_axis=0, tiled=True)

    grad, token = call(
        functools.partial(grad_body, rows, tiles, factor),
        (jax.ShapeDtypeStruct((size, LANES), F32), jax.ShapeDtypeStruct((8, LANES), F32)),
        [SMEM] * 2 + vmem(8),
        [work],
        flops=GRAD_FLOPS,
        name="grad",
    )(
        diff_x,
        diff_y,
        alpha_tiles,
        land_mask,
        masked,
        members_far,
        halo_near,
        adjoint,
        adjoint_far,
        adjoint_near,
    )
    hofx = call(
        unpack_body,
        jax.ShapeDtypeStruct((1, obs_row.shape[0]), F32),
        [ANY] + vmem(2),
        name="unpack",
    )(token, info, returned)
    return untiled(grad, alpha.shape), hofx.reshape(-1)


def solution(mesh):
    return jax.shard_map(
        on_device,
        mesh=mesh,
        in_specs=(
            P("mem", None, "tile", None),
            P("mem", None, "tile", None),
            P("mem"),
            P("mem"),
            P("tile", None),
            P(("tile", "mem"), None),
            P(("tile", "mem")),
            P(("tile", "mem")),
            P(("tile", "mem")),
            P(None, ("tile", "mem")),
            P(("tile", "mem")),
            P(("tile", "mem")),
        ),
        out_specs=(P("mem", None, "tile", None), P(("tile", "mem"))),
        check_vma=False,
    )
```

```python
import functools
import math

import jax
import jax.numpy as jnp
from jax import lax
from jax.experimental import pallas as pl
from jax.experimental.pallas import tpu as pltpu
from jax.sharding import PartitionSpec as P

STEPS = 8
COMPS = 8
LANES = 128
HIGHEST = lax.Precision.HIGHEST
F32 = jnp.float32
BF16 = jnp.bfloat16
I16 = jnp.int16
PARTIAL_FLOPS = 10**11
GRAD_FLOPS = 10**11


def iota(shape, dim):
    return lax.broadcasted_iota(jnp.int32, shape, dim)


def call(body, out_shape, in_specs=None, scratch=(), flops=0, moved=0, name=None, mib=48):
    return pl.pallas_call(
        body,
        out_shape=out_shape,
        in_specs=in_specs,
        scratch_shapes=scratch,
        compiler_params=pltpu.CompilerParams(vmem_limit_bytes=mib * 2**20),
        cost_estimate=pl.CostEstimate(flops=flops, bytes_accessed=moved, transcendentals=0),
        name=name,
    )


VMEM = pl.BlockSpec(memory_space=pltpu.VMEM)
SMEM = pl.BlockSpec(memory_space=pltpu.SMEM)
ANY = pl.BlockSpec(memory_space=pl.ANY)


def vmem(count):
    return [VMEM] * count


def ranks(tile_row):
    count = tile_row.shape[1]
    along = jnp.broadcast_to(tile_row, (count, count))
    down = along.T
    i, j = iota((count, count), 0), iota((count, count), 1)
    same = along == down
    column = jnp.sum(jnp.where(same & (j < i), 1.0, 0.0), axis=1, keepdims=True)
    row = jnp.sum(jnp.where(same & (i < j), 1.0, 0.0), axis=0, keepdims=True)
    return column, row


def pack(tiles, slots, tile_row, data):
    count = tile_row.shape[1]
    column, unused = ranks(tile_row)
    width = COMPS * slots
    expand = jnp.where(iota((COMPS, width), 1) // slots == iota((COMPS, width), 0), 1.0, 0.0)
    data = lax.dot_general(
        data, expand, (((0,), (0,)), ((), ())), precision=HIGHEST, preferred_element_type=F32
    )
    slot = (iota((count, width), 1) % slots).astype(F32)
    data = jnp.where(column == slot, data, 0.0)
    choose = jnp.where(iota((tiles, count), 0).astype(F32) == tile_row, 1.0, 0.0)
    return jnp.dot(choose, data, precision=HIGHEST, preferred_element_type=F32)


def unpack_body(unused_ref, info_ref, back_ref, hofx_ref):
    tile_row = info_ref[0:1, :]
    row = info_ref[1:2, :]
    tiles, slots = back_ref.shape
    count = tile_row.shape[1]
    choose = jnp.where(iota((tiles, count), 0).astype(F32) == tile_row, 1.0, 0.0)
    found = lax.dot_general(
        back_ref[...], choose, (((0,), (0,)), ((), ())), precision=HIGHEST, preferred_element_type=F32
    )
    keep = iota((slots, count), 0).astype(F32) == row
    hofx_ref[...] = jnp.sum(jnp.where(keep, found, 0.0), axis=0, keepdims=True)


def rates(group, keep, rate_x_ref, rate_y_ref):
    first = iota((8, LANES), 0) < 4
    rx = jnp.where(first, rate_x_ref[2 * group], rate_x_ref[2 * group + 1])
    ry = jnp.where(first, rate_y_ref[2 * group], rate_y_ref[2 * group + 1])
    centre = 1.0 - 2.0 * rx - 2.0 * ry
    return [(centre * k, rx * k, ry * k) for k in keep]


def smooth_rows(work, rows, coefs, emit):
    total = rows + 2 * STEPS
    parts = work.shape[2] // LANES
    lane = iota((8, LANES), 1)
    at_left, at_right = lane == 0, lane == LANES - 1

    def load(r):
        return [work[r, :, j * LANES : (j + 1) * LANES] for j in range(parts)]

    for step in range(STEPS):
        before, here = load(step), load(step + 1)
        for r in range(step + 1, total - 1 - step):
            after = load(r + 1)
            centre, rx, ry = coefs[0 if r < STEPS else (2 if r >= STEPS + rows else 1)]
            right = [pltpu.roll(v, 1, 1) for v in here]
            left = [pltpu.roll(v, LANES - 1, 1) for v in here]
            new = []
            for j in range(parts):
                low = jnp.where(at_left, right[j - 1] if j > 0 else 0.0, right[j])
                high = jnp.where(at_right, left[j + 1] if j + 1 < parts else 0.0, left[j])
                new.append(centre * here[j] + rx * (low + high) + ry * (before[j] + after[j]))
            if step == STEPS - 1:
                emit(r - STEPS, new)
            else:
                for j in range(parts):
                    work[r, :, j * LANES : (j + 1) * LANES] = new[j]
            before, here = here, after


def tiled(x):
    columns = x.shape[-1]
    x = x.reshape(-1, 8, columns // LANES, LANES)
    return jnp.swapaxes(x, 1, 2).reshape(-1, LANES)


def untiled(x, shape):
    x = x.reshape(-1, shape[-1] // LANES, 8, LANES)
    return jnp.swapaxes(x, 1, 2).reshape(shape)


def at_fields(base, stride, group, r, j, parts):
    return pl.ds(base + group * 8 * stride + (r // 8 * parts + j) * 8 + r % 8, 8, stride=stride)


def odd_tile():
    return lax.rem(lax.axis_index("tile"), 2)


def keep_sides(tiles):
    place = lax.axis_index("tile")
    return jnp.where(place > 0, 1.0, 0.0), jnp.where(place < tiles - 1, 1.0, 0.0)


def prep_body(tiles, slots, levels, *refs):
    sources, (far_ref, far_members_ref, near_ref, sent_ref), buffers, (data_ref, sems) = (
        refs[:10],
        refs[10:14],
        refs[14:24],
        refs[24:],
    )
    copies = [
        pltpu.make_async_copy(source, target, sems.at[k])
        for k, (source, target) in enumerate(zip(sources, buffers))
    ]
    for copy in copies:
        copy.start()
    for copy in copies:
        copy.wait()
    alpha_ref, members_ref, land_ref, tile_ref, row_ref, col_ref, lev_ref, weights_ref, value_ref, rinv_ref = buffers
    members, unused, rows, columns = members_ref.shape
    parts = columns // LANES
    size, brim = rows * parts, STEPS * parts
    odd = odd_tile()
    land = land_ref[...].astype(F32)
    is_odd = jnp.broadcast_to(odd, (STEPS, columns)) == 1
    land_first, land_last = land[:STEPS], land[rows - STEPS :]
    land_far, land_near = jnp.where(is_odd, land_last, land_first), jnp.where(is_odd, land_first, land_last)
    count = members * levels
    for f in range(count):
        field = members_ref[f // levels, f % levels].astype(F32)
        first, last = field[:STEPS], field[rows - STEPS :]
        for ref, other, mask, top, start in (
            (far_ref, far_members_ref, land_far, jnp.where(is_odd, last, first), odd * (size - brim)),
            (near_ref, near_ref, land_near, jnp.where(is_odd, first, last), (1 - odd) * (size - brim)),
        ):
            value = mask * top
            for j in range(parts):
                lanes = slice(j * LANES, (j + 1) * LANES)
                at = pl.multiple_of(f * size + start + j * 8, 8)
                ref[f * brim + j * 8 : f * brim + j * 8 + 8, :] = mask[:, lanes] * alpha_ref[pl.ds(at, 8), :]
                at = (f if other is far_members_ref else count + f) * brim + j * 8
                other[at : at + 8, :] = value[:, lanes]
    tile_row = tile_ref[...].astype(F32)
    data_ref[0:1, :] = col_ref[...].astype(F32)
    data_ref[1:2, :] = (row_ref[...] * levels + lev_ref[...]).astype(F32)
    data_ref[2:6, :] = weights_ref[...]
    data_ref[6:7, :] = value_ref[...]
    data_ref[7:8, :] = rinv_ref[...]
    sent_ref[...] = pack(tiles, slots, tile_row, data_ref[...])


def mask_body(tile_ref, alpha_ref, members_ref, land_ref, own_ref, masked_ref, info_ref):
    tile_row = tile_ref[...].astype(F32)
    unused, rank = ranks(tile_row)
    info_ref[0:1, :] = tile_row
    info_ref[1:2, :] = rank
    members, levels, rows, columns = members_ref.shape
    parts = columns // LANES
    size = rows * parts
    land = land_ref[...].astype(F32)
    for f in range(members * levels):
        field = land * members_ref[f // levels, f % levels].astype(F32)
        for k in range(rows // 8):
            for j in range(parts):
                at = f * size + (k * parts + j) * 8
                mask = land[k * 8 : k * 8 + 8, j * LANES : (j + 1) * LANES]
                own_ref[at : at + 8, :] = mask * alpha_ref[at : at + 8, :]
                masked_ref[at : at + 8, :] = field[k * 8 : k * 8 + 8, j * LANES : (j + 1) * LANES]


def partial_body(rows, tiles, rate_x_ref, rate_y_ref, own_ref, far_ref, near_ref, members_ref, out_ref, work):
    parts = out_ref.shape[1] // LANES
    size, brim = rows * parts, STEPS * parts
    odd = odd_tile()
    far_at, near_at = odd * (rows + STEPS), (1 - odd) * (rows + STEPS)
    below, above = keep_sides(tiles)
    for group in range(2):
        for j in range(parts):
            lanes = slice(j * LANES, (j + 1) * LANES)
            for r in range(STEPS):
                work[far_at + r, :, lanes] = far_ref[at_fields(0, brim, group, r, j, parts), :]
                work[near_at + r, :, lanes] = near_ref[at_fields(0, brim, group, r, j, parts), :]
            for r in range(rows):
                work[STEPS + r, :, lanes] = own_ref[at_fields(0, size, group, r, j, parts), :]
        coefs = rates(group, (below, 1.0, above), rate_x_ref, rate_y_ref)

        def emit(r, new, group=group):
            terms = [new[j] * members_ref[at_fields(0, size, group, r, j, parts), :] for j in range(parts)]
            if group == 0:
                for j in range(parts):
                    out_ref[r * 8 : r * 8 + 8, j * LANES : (j + 1) * LANES] = terms[j]
                return
            lane, half = iota((8, LANES), 1), iota((8, LANES), 0) < 4
            sums = []
            for j in range(parts):
                both = terms[j] + out_ref[r * 8 : r * 8 + 8, j * LANES : (j + 1) * LANES]
                sums.append(both + pltpu.roll(both, 4, 0))
            left = [pltpu.roll(v, LANES - 1, 1) for v in sums]
            for j in range(parts):
                later = left[j + 1] if j + 1 < parts else left[j]
                shifted = jnp.where(lane == LANES - 1, later, left[j])
                out_ref[r * 8 : r * 8 + 8, j * LANES : (j + 1) * LANES] = jnp.where(
                    half, sums[j], shifted
                )

        smooth_rows(work, rows, coefs, emit)


def grad_body(
    rows,
    tiles,
    factor,
    rate_x_ref,
    rate_y_ref,
    alpha_ref,
    land_ref,
    members_ref,
    far_ref,
    near_ref,
    adjoint_ref,
    adjoint_far_ref,
    adjoint_near_ref,
    out_ref,
    token_ref,
    work,
):
    token_ref[...] = jnp.zeros_like(token_ref)
    parts = land_ref.shape[1] // LANES
    size, brim = rows * parts, STEPS * parts
    odd = odd_tile()
    far_at, near_at = odd * (rows + STEPS), (1 - odd) * (rows + STEPS)
    below, above = keep_sides(tiles)

    def twice(ref, r, lanes):
        four = ref[r * 4 : r * 4 + 4, lanes]
        return jnp.concatenate([four, four], axis=0)

    for group in range(2):
        for j in range(parts):
            lanes = slice(j * LANES, (j + 1) * LANES)
            for r in range(STEPS):
                at = at_fields(0, brim, group, r, j, parts)
                work[far_at + r, :, lanes] = far_ref[at, :] * twice(adjoint_far_ref, r, lanes)
                at = at_fields(16 * brim, brim, group, r, j, parts)
                work[near_at + r, :, lanes] = near_ref[at, :] * twice(adjoint_near_ref, r, lanes)
            for r in range(rows):
                own = members_ref[at_fields(0, size, group, r, j, parts), :]
                work[STEPS + r, :, lanes] = own * adjoint_ref[r * 8 : r * 8 + 8, lanes]
        coefs = rates(group, (below, 1.0, above), rate_x_ref, rate_y_ref)

        def emit(r, new, group=group):
            for j in range(parts):
                lanes = slice(j * LANES, (j + 1) * LANES)
                land = jnp.broadcast_to(land_ref[r : r + 1, lanes].astype(F32), (8, LANES)) * factor
                at = at_fields(0, size, group, r, j, parts)
                out_ref[at, :] = alpha_ref[at, :] + land * new[j]

        smooth_rows(work, rows, coefs, emit)


def corner_terms(s, slots, comps, scale):
    def comp(k):
        return comps[k * slots + s : k * slots + s + 1, :]

    count = comps.shape[1]
    code = comp(1)
    level = code - 4.0 * jnp.floor(code * 0.25)
    row = jnp.floor(code * 0.25)
    sub = iota((8, count), 0).astype(F32)
    weights = [comp(2 + k) if scale is None else comp(2 + k) * scale for k in range(4)]
    left, right = sub == level, sub == level + 4.0
    lower = jnp.where(left, weights[0], jnp.where(right, weights[1], 0.0))
    upper = jnp.where(left, weights[2], jnp.where(right, weights[3], 0.0))
    return jnp.broadcast_to(row, (8, count)), lower, upper


def interpolate_body(rows, slots, raw_ref, field_ref, comps_ref, out_ref, pieces):
    comps_ref[...] = raw_ref[...].T
    columns = field_ref.shape[1]
    count = comps_ref.shape[1]
    field = field_ref[...]
    top = field.astype(BF16)
    pieces[: 8 * rows, :] = top
    pieces[8 * rows :, :] = (field - top.astype(F32)).astype(BF16)
    for s in range(slots):
        column = comps_ref[s : s + 1, :].astype(jnp.int32).astype(I16)
        hot = jnp.where(iota((columns, count), 0).astype(I16) == column, BF16(1.0), BF16(0.0))
        found = jnp.dot(pieces[...], hot, preferred_element_type=F32)
        row, lower, upper = corner_terms(s, slots, comps_ref, None)
        total = jnp.zeros((8, count), F32)
        previous = None
        for g in range(rows):
            at = row == float(g)
            value = found[g * 8 : g * 8 + 8] + found[8 * (rows + g) : 8 * (rows + g) + 8]
            rest = 0.0 if previous is None else jnp.where(previous, upper, 0.0)
            total = total + jnp.where(at, lower, rest) * value
            previous = at
        total = jnp.sum(total, axis=0, keepdims=True)
        for k in range(out_ref.shape[0]):
            out_ref[k, s : s + 1, :] = total


def copies_body(unused_ref, in_ref, out_ref):
    for k in range(out_ref.shape[0]):
        out_ref[k] = in_ref[...]


def add_body(in_ref, out_ref):
    total = in_ref[0]
    for k in range(1, in_ref.shape[0]):
        total = total + in_ref[k]
    for k in range(out_ref.shape[0]):
        out_ref[k] = total


def spread_scratch(rows, count, columns):
    return [
        pltpu.VMEM((16 * rows, count), BF16),
        pltpu.VMEM((count, columns), BF16),
        pltpu.VMEM((16 * rows, columns), F32),
    ]


def spread_body(
    rows, slots, tiles, factor, raw_ref, comps_ref, sums_ref, own_ref, far_ref, near_ref, back_ref, left, hot, total
):
    columns = own_ref.shape[1]
    count = comps_ref.shape[1]
    hofx = sums_ref[0]
    for k in range(1, sums_ref.shape[0]):
        hofx = hofx + sums_ref[k]
    hofx = factor * hofx
    mine = iota((tiles, count), 1) == lax.axis_index("mem") * tiles + iota((tiles, count), 0)
    back_ref[...] = lax.dot_general(
        jnp.where(mine, 1.0, 0.0),
        hofx,
        (((1,), (1,)), ((), ())),
        precision=HIGHEST,
        preferred_element_type=F32,
    )
    value = comps_ref[6 * slots : 7 * slots, :]
    rinv = comps_ref[7 * slots : 8 * slots, :]
    dep = rinv * (hofx - value)
    for s in range(slots):
        row, lower, upper = corner_terms(s, slots, comps_ref, dep[s : s + 1, :])
        previous, terms = None, []
        for g in range(rows):
            at = row == float(g)
            rest = 0.0 if previous is None else jnp.where(previous, upper, 0.0)
            terms.append(jnp.where(at, lower, rest))
            previous = at
            if g % 2 == 1:
                pair = jnp.concatenate(terms[-2:], axis=0)
                top = pair.astype(BF16)
                left[g * 8 - 8 : g * 8 + 8, :] = top
                left[8 * (rows + g) - 8 : 8 * (rows + g) + 8, :] = (pair - top.astype(F32)).astype(BF16)
        column = jnp.broadcast_to(raw_ref[:, s : s + 1].astype(jnp.int32), (count, LANES)).astype(I16)
        lane16 = iota((count, LANES), 1).astype(I16)
        for j in range(columns // LANES):
            lanes = slice(j * LANES, (j + 1) * LANES)
            hot[:, lanes] = jnp.where(lane16 + I16(j * LANES) == column, BF16(1.0), BF16(0.0))
        part = jnp.dot(left[...], hot[...], preferred_element_type=F32)
        if s == 0:
            total[...] = part
        else:
            total[...] += part
    lane, half = iota((8, columns), 1), iota((8, columns), 0) < 4
    for g in range(rows):
        both = total[g * 8 : g * 8 + 8, :] + total[8 * (rows + g) : 8 * (rows + g) + 8, :]
        moved = jnp.where(lane == 0, 0.0, pltpu.roll(pltpu.roll(both, 4, 0), 1, 1))
        four = both + moved
        own_ref[g * 8 : g * 8 + 8, :] = jnp.where(half, four, pltpu.roll(four, 4, 0))
    odd = odd_tile()
    first, last = odd * (rows - STEPS), (1 - odd) * (rows - STEPS)
    for ref, start in ((far_ref, first), (near_ref, last)):
        for r in range(STEPS):
            ref[r * 4 : r * 4 + 4, :] = own_ref[pl.ds(pl.multiple_of((start + r) * 8, 8), 8), :][:4]


def on_device(
    alpha,
    perturbs,
    diff_x,
    diff_y,
    land_mask,
    obs_tile,
    obs_row,
    obs_col,
    obs_lev,
    obs_weights,
    obs_value,
    obs_rinv,
):
    members, levels, rows, columns = alpha.shape
    tiles, mems = lax.axis_size("tile"), lax.axis_size("mem")
    factor = (mems * members - 1) ** (-0.5)
    slots = 16
    inner = math.isqrt(mems)
    near_group = [[i * inner + j for j in range(inner)] for i in range(inner)]
    far_group = [[i * inner + j for i in range(inner)] for j in range(inner)]
    pairs = [(i, i + 1) for i in range(0, tiles - 1, 2)]
    near_pairs = pairs + [(b, a) for a, b in pairs]
    pairs = [(i, i + 1) for i in range(1, tiles - 1, 2)]
    far_pairs = pairs + [(b, a) for a, b in pairs]
    size = members * levels * rows * columns // LANES
    brim = members * levels * STEPS * columns // LANES

    def to_far(x):
        return lax.ppermute(x, "tile", far_pairs)

    def to_near(x):
        return lax.ppermute(x, "tile", near_pairs)

    alpha_tiles = tiled(alpha)
    count = obs_row.shape[0]
    width = COMPS * slots
    sources = (
        alpha_tiles,
        perturbs,
        land_mask,
        obs_tile.reshape(1, count),
        obs_row.reshape(1, count),
        obs_col.reshape(1, count),
        obs_lev.reshape(1, count),
        obs_weights,
        obs_value.reshape(1, count),
        obs_rinv.reshape(1, count),
    )
    far, far_members, near, sent = call(
        functools.partial(prep_body, tiles, slots, levels),
        (
            jax.ShapeDtypeStruct((brim, LANES), F32),
            jax.ShapeDtypeStruct((brim, LANES), F32),
            jax.ShapeDtypeStruct((2 * brim, LANES), F32),
            jax.ShapeDtypeStruct((tiles, width), F32),
        ),
        [ANY] * len(sources),
        [pltpu.VMEM(x.shape, x.dtype) for x in sources]
        + [pltpu.VMEM((COMPS, count), F32), pltpu.SemaphoreType.DMA((len(sources),))],
        name="prep",
        mib=60,
    )(*sources)
    halo_far, halo_near, members_far = to_far(far), to_near(near), to_far(far_members)
    routed = lax.all_to_all(sent, "tile", split_axis=0, concat_axis=0, tiled=True)
    own, masked, info = call(
        mask_body,
        (
            jax.ShapeDtypeStruct((size, LANES), F32),
            jax.ShapeDtypeStruct((size, LANES), F32),
            jax.ShapeDtypeStruct((2, count), F32),
        ),
        vmem(4),
        name="mask",
    )(sources[3], alpha_tiles, perturbs, land_mask)
    count = mems * tiles
    work = pltpu.VMEM((rows + 2 * STEPS, 8, columns), F32)
    partial = call(
        functools.partial(partial_body, rows, tiles),
        jax.ShapeDtypeStruct((8 * rows, columns), F32),
        [SMEM] * 2 + vmem(4),
        [work],
        flops=PARTIAL_FLOPS,
        name="partial",
    )(diff_x, diff_y, own, halo_far, halo_near, masked)
    copied = call(
        copies_body,
        jax.ShapeDtypeStruct((mems, tiles, width), F32),
        [ANY] + vmem(1),
        name="copies",
    )(partial, routed)
    raw = lax.all_to_all(copied, "mem", split_axis=0, concat_axis=0, tiled=True).reshape(count, width)
    copies = jax.ShapeDtypeStruct((inner, slots, count), F32)
    comps, found = call(
        functools.partial(interpolate_body, rows, slots),
        (jax.ShapeDtypeStruct((width, count), F32), copies),
        vmem(2),
        [pltpu.VMEM((16 * rows, columns), BF16)],
        name="interpolate",
    )(raw, partial)

    def gather(x, groups):
        return lax.all_to_all(x, "mem", split_axis=0, concat_axis=0, axis_index_groups=groups, tiled=True)

    sums = gather(call(add_body, copies, vmem(1), name="add")(gather(found, near_group)), far_group)
    edge = jax.ShapeDtypeStruct((levels * STEPS, columns), F32)
    adjoint, edge_far, edge_near, back = call(
        functools.partial(spread_body, rows, slots, tiles, factor),
        (
            jax.ShapeDtypeStruct((8 * rows, columns), F32),
            edge,
            edge,
            jax.ShapeDtypeStruct((tiles, slots), F32),
        ),
        vmem(3),
        spread_scratch(rows, count, columns),
        name="spread",
    )(raw, comps, sums)
    adjoint_far = to_far(edge_far)
    adjoint_near = to_near(edge_near)
    returned = lax.all_to_all(back, "tile", split_axis=0, concat_axis=0, tiled=True)

    grad, token = call(
        functools.partial(grad_body, rows, tiles, factor),
        (jax.ShapeDtypeStruct((size, LANES), F32), jax.ShapeDtypeStruct((8, LANES), F32)),
        [SMEM] * 2 + vmem(8),
        [work],
        flops=GRAD_FLOPS,
        name="grad",
    )(
        diff_x,
        diff_y,
        alpha_tiles,
        land_mask,
        masked,
        members_far,
        halo_near,
        adjoint,
        adjoint_far,
        adjoint_near,
    )
    hofx = call(
        unpack_body,
        jax.ShapeDtypeStruct((1, obs_row.shape[0]), F32),
        [ANY] + vmem(2),
        name="unpack",
    )(token, info, returned)
    return untiled(grad, alpha.shape), hofx.reshape(-1)


def solution(mesh):
    return jax.shard_map(
        on_device,
        mesh=mesh,
        in_specs=(
            P("mem", None, "tile", None),
            P("mem", None, "tile", None),
            P("mem"),
            P("mem"),
            P("tile", None),
            P(("tile", "mem"), None),
            P(("tile", "mem")),
            P(("tile", "mem")),
            P(("tile", "mem")),
            P(None, ("tile", "mem")),
            P(("tile", "mem")),
            P(("tile", "mem")),
        ),
        out_specs=(P("mem", None, "tile", None), P(("tile", "mem"))),
        check_vma=False,
    )
```
